512 devices in a mesh: row: 16 (over x, z_lo), col: 32 (over z_hi, y, core).
Axes of the slice: x: 4, y: 4, z: 16 (z_hi: 4, z_lo: 4; z = z_hi * 4 + z_lo), core: 2. Of those that a mesh axis runs over, the one named last changes fastest.
Arguments:
- covariance: float32 [16384, 16384], P('row', 'col')
- angles: float32 [3, 8192], replicated, may hold values from 0.3 to 1.3
- delays: int32 [3], replicated, may hold values from 128 to 8192, as said below
- panel: int32 [1], replicated, may hold values from 0 to 8064
Outputs:
- conditioned: float32 [16384, 16384], P('row', 'col')
The draws below stay inside these ranges and needn't reach their ends.
Inputs may be any that keep to these rules, and one draw needn't show every extreme that they name: `delays`: each delay is 128 times a power of two; one of the three is 128, one is 8192.
All inputs are finite; a program needn't handle non-finite values.
Results may differ from the reference program's by a relative error of at most 0.000094.
Values sent between devices are 32-bit elements; how exact they have to be, the bound alone decides.
No kernel may reach another device: no remote copies, remote signals or barrier semaphores. Data moves between devices by JAX's collectives and lax.ppermute only.
A program may use at most 64 MiB of HBM per device.

```python
import jax
import jax.numpy as jnp
from jax import lax

PANEL = 128
N = 16384
MODES = 8192


def draw_covariance(key, part):
    key = jax.random.fold_in(key, 11)
    key_off = jax.random.fold_in(key, 0)
    key_diag = jax.random.fold_in(key, 1)
    key_factor = jax.random.fold_in(key, 3)
    rank_count = 128
    raw = jax.random.normal(key_off, (N, N), jnp.float32)
    factors = jax.random.normal(key_factor, (N, rank_count), jnp.float32)
    spread = 1.5 / jnp.sqrt(2.0 * N)
    off = (raw + raw.T) * spread
    diag_vals = jax.random.uniform(key_diag, (N,), jnp.float32, 4.5, 9.0)
    row_ids = jnp.arange(N, dtype=jnp.int32)
    base = jnp.where(row_ids[:, None] == row_ids[None, :], diag_vals[:, None], off)
    shared = jnp.dot(factors, factors.T, precision=lax.Precision.HIGHEST) * (1.5 / rank_count)
    total = base + shared
    return (0.5 * (total + total.T)).astype(jnp.float32)


def draw_delays(key, part):
    key = jax.random.fold_in(key, 23)
    key_level, key_order = jax.random.split(key)
    levels = (N // 256).bit_length()
    level = jax.random.randint(key_level, (), 0, levels)
    third = jnp.left_shift(jnp.int32(128), level.astype(jnp.int32))
    values = jnp.stack([jnp.int32(N // 2), jnp.int32(128), third]).astype(jnp.int32)
    order = jax.random.permutation(key_order, 3)
    return jnp.take(values, order).astype(jnp.int32)


def setup_inputs(seed: int = 0) -> dict:
    key_of = jax.random.split(jax.random.key(seed), 5)
    covariance = draw_covariance(jax.random.fold_in(key_of[4], 71), 0)
    angles = jnp.clip(jax.random.uniform(key_of[1], (3, MODES), jnp.float32, 0.3, 1.3), 0.3, 1.3)
    delays = draw_delays(jax.random.fold_in(key_of[4], 71), 0)
    panel = jax.random.randint(key_of[3], (1,), 0, MODES - PANEL + 1).astype(jnp.int32)
    return dict(covariance=covariance, angles=angles, delays=delays, panel=panel)


def coefficients(angle_row, delay, index):
    low = index // delay % 2 == 0
    source = jnp.where(low, index, index - delay).astype(jnp.int32)
    theta = angle_row[source % MODES]
    own = jnp.cos(theta)
    other = jnp.where(low, -jnp.sin(theta), jnp.sin(theta))
    partner = jnp.where(low, index + delay, index - delay).astype(jnp.int32)
    return (own, other, partner)

def reference(covariance, angles, delays, panel):
    field = covariance
    index = jnp.arange(N, dtype=jnp.int32)
    for section in range(3):
        own, other, partner = coefficients(angles[section], delays[section], index)
        field = own[:, None] * field + other[:, None] * field[partner, :]
        field = field * own[None, :] + field[:, partner] * other[None, :]
    start = panel[0]
    slots = jnp.arange(2 * PANEL, dtype=jnp.int32)
    chosen = jnp.where(slots < PANEL, start + slots, MODES + start + slots - PANEL).astype(jnp.int32)
    columns = field[:, chosen]
    rows_part = field[chosen, :]
    block = rows_part[:, chosen]
    factor = jnp.linalg.cholesky(block)
    half = lax.linalg.triangular_solve(factor, rows_part, left_side=True, lower=True)
    weights = lax.linalg.triangular_solve(factor, half, left_side=True, lower=True, transpose_a=True)
    return field - jnp.dot(columns, weights, precision=lax.Precision.HIGHEST)
```

```python
import functools

import jax
import jax.numpy as jnp
from jax import lax
from jax.experimental import pallas as pl
from jax.experimental.pallas import tpu as pltpu
from jax.sharding import PartitionSpec as P

PANEL = 128
QUANTUM = 128
HIGHEST = lax.Precision.HIGHEST
VMEM = pl.BlockSpec(memory_space=pltpu.VMEM)
SMEM = pl.BlockSpec(memory_space=pltpu.SMEM)


def swap(value, axis, mask):
    pairs = [(source, source ^ mask) for source in range(lax.axis_size(axis))]
    return lax.ppermute(value, axis, pairs)


class Plan:
    def __init__(self, level, top, row_blocks, col_blocks):
        self.gens = sorted({1, 1 << level, top})
        self.third = 1 << level
        self.top = top
        self.count = 1 << len(self.gens)
        self.top_bit = 1 << self.gens.index(top)
        self.third_bit = 1 << self.gens.index(self.third)
        self.values = [
            sum(g for k, g in enumerate(self.gens) if m >> k & 1) for m in range(self.count)
        ]
        self.row_blocks = row_blocks
        self.col_blocks = col_blocks
        inner = self.third not in (1, top)
        self.row_far = inner and self.third >= row_blocks
        self.col_far = inner and self.third >= col_blocks


def coefficients_kernel(plan, info, angles, out):
    count, top = plan.count, plan.top
    rows = 16 * count
    rid = lax.broadcasted_iota(jnp.int32, (rows, top), 0)
    lane = lax.broadcasted_iota(jnp.int32, (rows, top), 1)
    slot = rid & 15
    base = jnp.where(slot < 8, info[3] + slot, info[4] + (slot & (plan.col_blocks - 1)))
    mask = jnp.zeros_like(rid)
    for k, g in enumerate(plan.gens):
        mask = mask | (((rid >> (4 + k)) & 1) * g)
    block = base ^ mask
    own, other, delays = [], [], []
    for section in range(3):
        d = info[section]
        source = (block & ~d) & (top - 1)
        pick = (source == lane).astype(jnp.float32)
        theta = angles[section * top : (section + 1) * top, :]
        low = (block[:, :1] & d) == 0
        cos = jnp.dot(pick, jnp.cos(theta), precision=HIGHEST, preferred_element_type=jnp.float32)
        sin = jnp.dot(pick, jnp.sin(theta), precision=HIGHEST, preferred_element_type=jnp.float32)
        sin = jnp.where(low, -sin, sin)
        own.append([cos[16 * m : 16 * m + 16] for m in range(count)])
        other.append([sin[16 * m : 16 * m + 16] for m in range(count)])
        delays.append(d)

    def partner(values, d, m):
        result = values[m ^ 1]
        for k, g in enumerate(plan.gens[1:], 1):
            result = jnp.where(d == g, values[m ^ (1 << k)], result)
        return result

    one = jnp.ones((16, 128), jnp.float32)
    zero = jnp.zeros((16, 128), jnp.float32)

    def row_of(start):
        values = [one if m == start else zero for m in range(count)]
        for section in (2, 1, 0):
            a, b, d = own[section], other[section], delays[section]
            scaled = [values[m] * b[m] for m in range(count)]
            values = [values[m] * a[m] + partner(scaled, d, m) for m in range(count)]
        return values

    def col_of():
        values = [one if m == 0 else zero for m in range(count)]
        for section in (0, 1, 2):
            a, b, d = own[section], other[section], delays[section]
            values = [values[m] * a[m] + b[m] * partner(values, d, m) for m in range(count)]
        return values

    for n, values in enumerate(
        (row_of(0), row_of(plan.top_bit), col_of(), row_of(plan.third_bit))
    ):
        for m in range(count):
            out[n, m] = values[m]


def coefficients(plan, info, angles):
    return pl.pallas_call(
        functools.partial(coefficients_kernel, plan),
        out_shape=jax.ShapeDtypeStruct((4, plan.count, 16, 128), jnp.float32),
        in_specs=[SMEM, VMEM],
        out_specs=VMEM,
        compiler_params=pltpu.CompilerParams(vmem_limit_bytes=32 * 2**20),
    )(info, angles)


def row_kernel(plan, height, near_ref, top_ref, coef_ref, *outs):
    tables = [coef_ref[0], coef_ref[3]] if plan.row_far else [coef_ref[0]]
    blocks = height // 128
    far = plan.third_bit if plan.row_far else 0
    for which, out in enumerate(outs):
        table = tables[which]
        columns = [jnp.transpose(table[m, :8, :]) for m in range(plan.count)]
        for j in range(blocks):
            total = None
            for m in range(plan.count):
                if m & far:
                    continue
                ref = top_ref if m & plan.top_bit else near_ref
                value = plan.values[m] & ~plan.top
                i = j ^ value
                term = ref[128 * i : 128 * i + 128, :] * columns[m][:, j : j + 1]
                total = term if total is None else total + term
            out[128 * j : 128 * j + 128, :] = total


def mix_rows(plan, near, top, coef, width=128):
    height, all_width = near.shape
    n_out = 2 if plan.row_far else 1
    block = pl.BlockSpec((height, width), lambda i: (0, i))
    shape = jax.ShapeDtypeStruct(near.shape, jnp.float32)
    return pl.pallas_call(
        functools.partial(row_kernel, plan, height),
        grid=(all_width // width,),
        out_shape=[shape] * n_out,
        in_specs=[block, block, VMEM],
        out_specs=[block] * n_out,
        compiler_params=pltpu.CompilerParams(vmem_limit_bytes=48 * 2**20),
    )(near, top, coef)


def col_kernel(plan, *refs):
    if plan.col_far:
        near_ref, far_ref, coef_ref, mine, theirs = refs
    else:
        near_ref, coef_ref, mine, theirs = refs
        far_ref = None
    far = plan.third_bit if plan.col_far else 0
    for which, out in enumerate((mine, theirs)):
        for j in range(plan.col_blocks):
            total = None
            for m in range(plan.count):
                if m & plan.top_bit:
                    continue
                ref = far_ref if m & far else near_ref
                value = plan.values[m] & ~(plan.third if m & far else 0)
                i = j ^ value
                term = ref[:, 128 * i : 128 * i + 128] * coef_ref[which, m, 8 + j : 9 + j, :]
                total = term if total is None else total + term
            out[:, 128 * j : 128 * j + 128] = total


def mix_cols(plan, parts, coef, strip=128):
    height, width = parts[0].shape
    block = pl.BlockSpec((strip, width), lambda i: (i, 0))
    shape = jax.ShapeDtypeStruct((height, width), jnp.float32)
    return pl.pallas_call(
        functools.partial(col_kernel, plan),
        grid=(height // strip,),
        out_shape=[shape] * 2,
        in_specs=[block] * len(parts) + [VMEM],
        out_specs=[block] * 2,
        compiler_params=pltpu.CompilerParams(vmem_limit_bytes=48 * 2**20),
    )(*parts, coef)


def selection(plan, coef, base, n_blocks, first, panel, modes):
    n = n_blocks * QUANTUM
    ids = base * QUANTUM + jnp.arange(n, dtype=jnp.int32)
    slots = jnp.arange(2 * PANEL, dtype=jnp.int32)
    chosen = jnp.where(slots < PANEL, panel + slots, modes + panel + slots - PANEL)
    result = jnp.zeros((2 * PANEL, n), jnp.float32)
    for m in range(plan.count):
        at = ids ^ (plan.values[m] * QUANTUM)
        weight = coef[2, m, first : first + n_blocks].reshape(n)
        result = result + jnp.where(at[None, :] == chosen[:, None], weight[None, :], 0.0)
    return result


def gather_four(value, axis, unit):
    place = lax.axis_index(axis) // unit % 4
    result = jnp.zeros((4,) + value.shape, value.dtype)
    moved = [value] + [swap(value, axis, unit * k) for k in (1, 2, 3)]
    for k, piece in enumerate(moved):
        result = lax.dynamic_update_slice(result, piece[None], (place ^ k,) + (0,) * value.ndim)
    return result


def transposed(value):
    n_row, n_col = lax.axis_size("row"), lax.axis_size("col")
    pairs = []
    for r in range(n_row):
        for c in range(n_col):
            pairs.append((r * n_col + c, (c // 2) * n_col + r * 2 + c % 2))
    return lax.ppermute(value, ("row", "col"), pairs)


def panel_rows(plan, covariance, coef, rb, cb, panel, modes):
    rows_dev, cols_dev = covariance.shape
    n_row = lax.axis_size("row")
    sel_r = selection(plan, coef, rb, plan.row_blocks, 0, panel, modes)
    sel_c = selection(plan, coef, cb, plan.col_blocks, 8, panel, modes)
    part = jnp.dot(sel_r, covariance, precision=HIGHEST)
    each = 2 * PANEL // n_row
    spread = lax.all_to_all(part.reshape(n_row, each, cols_dev), "row", 0, 0)
    piece = jnp.sum(spread, axis=0)
    block = jnp.dot(piece, sel_c.T, precision=HIGHEST)
    block = block + swap(block, "col", 1)
    block = sum([swap(block, "col", 2 * k) for k in (1, 2, 3)], block)
    block = sum([swap(block, "col", 8 * k) for k in (1, 2, 3)], block)
    moved = {0: piece, plan.top_bit: swap(piece, "col", plan.top // plan.col_blocks)}
    if plan.col_far:
        mask = plan.third // plan.col_blocks
        moved[plan.third_bit] = swap(piece, "col", mask)
        both = mask ^ (plan.top // plan.col_blocks)
        moved[plan.third_bit | plan.top_bit] = swap(piece, "col", both)
    far = plan.top_bit | (plan.third_bit if plan.col_far else 0)
    far_value = plan.top | (plan.third if plan.col_far else 0)
    mixed = []
    for j in range(plan.col_blocks):
        total = 0.0
        for m in range(plan.count):
            i = j ^ (plan.values[m] & ~far_value)
            source = moved[m & far][:, 128 * i : 128 * i + 128]
            total = total + source * coef[0, m, 8 + j][None, :]
        mixed.append(total)
    mixed = jnp.concatenate(mixed, axis=1)
    return block, mixed


def branch(level, covariance, angles, delays, panel):
    rows_dev, cols_dev = covariance.shape
    n_row, n_col = lax.axis_size("row"), lax.axis_size("col")
    modes = rows_dev * n_row // 2
    top = modes // QUANTUM
    plan = Plan(level, top, rows_dev // QUANTUM, cols_dev // QUANTUM)
    row_top = top // plan.row_blocks
    rb = lax.axis_index("row").astype(jnp.int32) * plan.row_blocks
    cb = lax.axis_index("col").astype(jnp.int32) * plan.col_blocks
    info = jnp.concatenate([delays // QUANTUM, rb[None], cb[None]]).astype(jnp.int32)
    coef = coefficients(plan, info, angles.reshape(3 * top, QUANTUM))
    over = swap(covariance, "row", row_top)

    block, mixed = panel_rows(plan, covariance, coef, rb, cb, panel, modes)

    if plan.row_far:
        mine, theirs = mix_rows(plan, covariance, over, coef)
        field = mine + swap(theirs, "row", plan.third // plan.row_blocks)
    else:
        (field,) = mix_rows(plan, covariance, over, coef)
    parts = [field]
    if plan.col_far:
        parts.append(swap(field, "col", plan.third // plan.col_blocks))
    mine, theirs = mix_cols(plan, parts, coef)
    arrived = swap(theirs, "col", top // plan.col_blocks)

    each = mixed.shape[0]
    both = jnp.concatenate([mixed, block], axis=1)
    both = lax.all_to_all(jnp.broadcast_to(both[None], (n_row,) + both.shape), "row", 0, 0)
    both = both.reshape(2 * PANEL, -1)
    rows_part, square = both[:, :cols_dev], both[:, cols_dev:]
    flipped = transposed(mixed)
    flipped = gather_four(flipped, "col", 8)
    flipped = gather_four(flipped, "col", 2)
    core = lax.axis_index("col") % 2
    twin = swap(flipped, "col", 1)
    pair = jnp.zeros(flipped.shape[:3] + (2, cols_dev), jnp.float32)
    pair = lax.dynamic_update_slice(pair, flipped[:, :, :, None], (0, 0, 0, core, 0))
    pair = lax.dynamic_update_slice(pair, twin[:, :, :, None], (0, 0, 0, 1 - core, 0))
    columns = pair.transpose(1, 0, 2, 3, 4).reshape(2 * PANEL, rows_dev)

    factor = jnp.linalg.cholesky(square)
    half = lax.linalg.triangular_solve(factor, rows_part, left_side=True, lower=True)
    weights = lax.linalg.triangular_solve(
        factor, half, left_side=True, lower=True, transpose_a=True
    )
    update = lax.dot_general(columns, weights, (((0,), (0,)), ((), ())), precision=HIGHEST)
    return mine + arrived - update


def shards(covariance, angles, delays, panel):
    rows_dev = covariance.shape[0]
    modes = rows_dev * lax.axis_size("row") // 2
    levels = (modes // QUANTUM).bit_length()
    third = jnp.sum(delays) - modes - QUANTUM
    level = jnp.int32(0)
    for n in range(1, levels):
        level = level + (third >= QUANTUM * (1 << n)).astype(jnp.int32)
    branches = [functools.partial(branch, n) for n in range(levels)]
    return lax.switch(level, branches, covariance, angles, delays, panel[0])


def solution(mesh):
    in_specs = (P("row", "col"), P(), P(), P())
    out_specs = P("row", "col")
    return jax.shard_map(shards, mesh=mesh, in_specs=in_specs, out_specs=out_specs, check_vma=False)
```

```python
import functools

import jax
import jax.numpy as jnp
from jax import lax
from jax.experimental import pallas as pl
from jax.experimental.pallas import tpu as pltpu
from jax.sharding import PartitionSpec as P

PANEL = 128
QUANTUM = 128
HIGHEST = lax.Precision.HIGHEST
VMEM = pl.BlockSpec(memory_space=pltpu.VMEM)
SMEM = pl.BlockSpec(memory_space=pltpu.SMEM)


def swap(value, axis, mask):
    pairs = [(source, source ^ mask) for source in range(lax.axis_size(axis))]
    return lax.ppermute(value, axis, pairs)


def swap_far(value, axis, third, thirds, per_device):
    if len(thirds) == 1:
        return swap(value, axis, thirds[0] // per_device)
    index = sum((third > t).astype(jnp.int32) for t in thirds[:-1])
    ways = [functools.partial(swap, axis=axis, mask=t // per_device) for t in thirds]
    return lax.switch(index, ways, value)


class Plan:
    count, third_bit, top_bit = 8, 2, 4

    def __init__(self, thirds, top, row_blocks, col_blocks):
        third = thirds[0]
        self.third, self.thirds, self.top = third, thirds, top
        self.values = [(m & 1) + (m >> 1 & 1) * third + (m >> 2) * top for m in range(self.count)]
        self.row_blocks = row_blocks
        self.col_blocks = col_blocks
        self.row_far = third >= row_blocks
        self.col_far = third >= col_blocks


def coefficients_kernel(count, top, col_blocks, info, angles, out):
    gens = (1, info[5], top)
    rows = 16 * count
    rid = lax.broadcasted_iota(jnp.int32, (rows, top), 0)
    lane = lax.broadcasted_iota(jnp.int32, (rows, top), 1)
    slot = rid & 15
    base = jnp.where(slot < 8, info[3] + slot, info[4] + (slot & (col_blocks - 1)))
    mask = jnp.zeros_like(rid)
    for k, g in enumerate(gens):
        mask = mask | (((rid >> (4 + k)) & 1) * g)
    block = base ^ mask
    own, other, delays = [], [], []
    for section in range(3):
        d = info[section]
        source = (block & ~d) & (top - 1)
        pick = (source == lane).astype(jnp.float32)
        theta = angles[section * top : (section + 1) * top, :]
        low = (block[:, :1] & d) == 0
        cos = jnp.dot(pick, jnp.cos(theta), precision=HIGHEST, preferred_element_type=jnp.float32)
        sin = jnp.dot(pick, jnp.sin(theta), precision=HIGHEST, preferred_element_type=jnp.float32)
        sin = jnp.where(low, -sin, sin)
        own.append([cos[16 * m : 16 * m + 16] for m in range(count)])
        other.append([sin[16 * m : 16 * m + 16] for m in range(count)])
        delays.append(d)

    def partner(values, d, m):
        result = values[m ^ 1]
        for k, g in enumerate(gens[1:], 1):
            result = jnp.where(d == g, values[m ^ (1 << k)], result)
        return result

    one = jnp.ones((16, 128), jnp.float32)
    zero = jnp.zeros((16, 128), jnp.float32)

    def row_of(start):
        values = [one if m == start else zero for m in range(count)]
        for section in (2, 1, 0):
            a, b, d = own[section], other[section], delays[section]
            scaled = [values[m] * b[m] for m in range(count)]
            values = [values[m] * a[m] + partner(scaled, d, m) for m in range(count)]
        return values

    def col_of():
        values = [one if m == 0 else zero for m in range(count)]
        for section in (0, 1, 2):
            a, b, d = own[section], other[section], delays[section]
            values = [values[m] * a[m] + b[m] * partner(values, d, m) for m in range(count)]
        return values

    for n, values in enumerate(
        (row_of(0), row_of(Plan.top_bit), col_of(), row_of(Plan.third_bit))
    ):
        for m in range(count):
            out[n, m] = values[m]


def coefficients(top, col_blocks, info, angles):
    return pl.pallas_call(
        functools.partial(coefficients_kernel, Plan.count, top, col_blocks),
        out_shape=jax.ShapeDtypeStruct((4, Plan.count, 16, 128), jnp.float32),
        in_specs=[SMEM, VMEM],
        out_specs=VMEM,
        compiler_params=pltpu.CompilerParams(vmem_limit_bytes=32 * 2**20),
    )(info, angles)


def row_kernel(plan, height, near_ref, top_ref, coef_ref, *outs, rows=slice(0, 8)):
    tables = [0, 3]
    blocks = height // 128
    far = plan.third_bit if plan.row_far else 0
    for which, out in enumerate(outs):
        table = tables[which]
        columns = [jnp.transpose(coef_ref[table, m, rows, :]) for m in range(plan.count)]
        for j in range(blocks):
            total = None
            for m in range(plan.count):
                if m & far:
                    continue
                ref = top_ref if m & plan.top_bit else near_ref
                value = plan.values[m] & ~plan.top
                i = j ^ value
                term = ref[128 * i : 128 * i + 128, :] * columns[m][:, j : j + 1]
                total = term if total is None else total + term
            out[128 * j : 128 * j + 128, :] = total


def mix_rows(plan, near, top, coef, width=128):
    height, all_width = near.shape
    n_out = 2 if plan.row_far else 1
    block = pl.BlockSpec((height, width), lambda i: (0, i))
    shape = jax.ShapeDtypeStruct(near.shape, jnp.float32)
    return pl.pallas_call(
        functools.partial(row_kernel, plan, height),
        grid=(all_width // width,),
        out_shape=[shape] * n_out,
        in_specs=[block, block, VMEM],
        out_specs=[block] * n_out,
        compiler_params=pltpu.CompilerParams(vmem_limit_bytes=48 * 2**20),
    )(near, top, coef)


def col_kernel(plan, *refs):
    if plan.col_far:
        near_ref, far_ref, coef_ref, mine, theirs = refs
    else:
        near_ref, coef_ref, mine, theirs = refs
        far_ref = None
    far = plan.third_bit if plan.col_far else 0
    for which, out in enumerate((mine, theirs)):
        for j in range(plan.col_blocks):
            total = None
            for m in range(plan.count):
                if m & plan.top_bit:
                    continue
                ref = far_ref if m & far else near_ref
                value = plan.values[m] & ~(plan.third if m & far else 0)
                i = j ^ value
                term = ref[:, 128 * i : 128 * i + 128] * coef_ref[which, m, 8 + j : 9 + j, :]
                total = term if total is None else total + term
            out[:, 128 * j : 128 * j + 128] = total


def mix_cols(plan, parts, coef, strip=128):
    height, width = parts[0].shape
    block = pl.BlockSpec((strip, width), lambda i: (i, 0))
    shape = jax.ShapeDtypeStruct((height, width), jnp.float32)
    return pl.pallas_call(
        functools.partial(col_kernel, plan),
        grid=(height // strip,),
        out_shape=[shape] * 2,
        in_specs=[block] * len(parts) + [VMEM],
        out_specs=[block] * 2,
        compiler_params=pltpu.CompilerParams(vmem_limit_bytes=48 * 2**20),
    )(*parts, coef)


def near_kernel(plan, height, near_ref, top_ref, coef_ref, mine, theirs, middle):
    blocks = height // 128
    start = pl.program_id(0) * blocks
    row_kernel(plan, height, near_ref, top_ref, coef_ref, middle, rows=pl.ds(start, blocks))
    col_kernel(plan, middle, coef_ref, mine, theirs)


def mix_near(plan, near, top, coef):
    height, width = near.shape
    half = height // 2
    block = pl.BlockSpec((half, width), lambda i: (i, 0))
    shape = jax.ShapeDtypeStruct((height, width), jnp.float32)
    return pl.pallas_call(
        functools.partial(near_kernel, plan, half),
        grid=(2,),
        out_shape=[shape] * 2,
        in_specs=[block, block, pl.BlockSpec(coef.shape[:2] + (16, 128), lambda i: (0, 0, 0, 0))],
        out_specs=[block] * 2,
        scratch_shapes=[pltpu.VMEM((half, width), jnp.float32)],
        compiler_params=pltpu.CompilerParams(vmem_limit_bytes=48 * 2**20),
    )(near, top, coef)


def dot(a, b, over=((1,), (0,))):
    return lax.dot_general(
        a, b, (over, ((), ())), precision=HIGHEST, preferred_element_type=jnp.float32
    )


def inverse_factor(block):
    n = block.shape[0]
    i = lax.broadcasted_iota(jnp.int32, (8, 2 * n), 0)
    lane = lax.broadcasted_iota(jnp.int32, (8, 2 * n), 1)
    unit = [jnp.where(lane == i + 8 * t + n, 1.0, 0.0) for t in range(n // 8)]
    wide = jnp.concatenate([block, jnp.zeros_like(block)], axis=1)
    tiles = [wide[8 * t : 8 * t + 8] + unit[t] for t in range(n // 8)]
    for j in range(n):
        first, r = divmod(j, 8)
        row = tiles[first][r : r + 1, :]
        scaled = row * (1.0 / row[:, j : j + 1])
        for t in range(first, n // 8):
            col = tiles[t][:, j : j + 1]
            if t == first:
                col = jnp.where(i[:, :1] > r, col, 0.0)
            tiles[t] = tiles[t] - col * scaled
    out = []
    for t in range(n // 8):
        pivot = jnp.sum(jnp.where(lane == i + 8 * t, tiles[t], 0.0), axis=1, keepdims=True)
        out.append(tiles[t][:, n:] * lax.rsqrt(pivot))
    return jnp.concatenate(out, axis=0)


def weights_kernel(square, given, out, work, right):
    size, n = square.shape[0], 64
    work[...] = square[...]
    right[...] = given[...]
    inverses = []
    for k in range(0, size, n):
        inverse = inverse_factor(work[k : k + n, k : k + n])
        inverses.append(inverse)
        mine = dot(inverse, right[k : k + n, :])
        right[k : k + n, :] = mine
        if k + n < size:
            below = dot(work[k + n :, k : k + n], inverse, ((1,), (1,)))
            work[k + n :, k : k + n] = below
            work[k + n :, k + n :] -= dot(below, below, ((1,), (1,)))
            right[k + n :, :] -= dot(below, mine)
    for k in range(size - n, -1, -n):
        rest = right[k : k + n, :]
        if k + n < size:
            rest = rest - dot(work[k + n :, k : k + n], out[k + n :, :], ((0,), (0,)))
        out[k : k + n, :] = dot(inverses[k // n], rest, ((0,), (0,)))


def solve_weights(square, given):
    return pl.pallas_call(
        weights_kernel,
        out_shape=jax.ShapeDtypeStruct(given.shape, jnp.float32),
        in_specs=[VMEM, VMEM],
        out_specs=VMEM,
        scratch_shapes=[
            pltpu.VMEM(square.shape, jnp.float32),
            pltpu.VMEM(given.shape, jnp.float32),
        ],
        compiler_params=pltpu.CompilerParams(vmem_limit_bytes=32 * 2**20),
    )(square, given)


def selection(coef, base, n_blocks, first, third, top, panel):
    n = n_blocks * QUANTUM
    ids = base * QUANTUM + jnp.arange(n, dtype=jnp.int32)
    slots = jnp.arange(2 * PANEL, dtype=jnp.int32)
    chosen = panel + jnp.where(slots < PANEL, slots, top * QUANTUM + slots - PANEL)
    result = jnp.zeros((2 * PANEL, n), jnp.float32)
    for m in range(Plan.count):
        at = ids ^ (((m & 1) + (m >> 1 & 1) * third + (m >> 2) * top) * QUANTUM)
        weight = coef[2, m, first : first + n_blocks].reshape(n)
        result = result + jnp.where(at[None, :] == chosen[:, None], weight[None, :], 0.0)
    return result


def gather_pairs(value):
    n_col = lax.axis_size("col")
    groups = [list(range(core, n_col, 2)) for core in (0, 1)]
    many = jnp.broadcast_to(value[None], (n_col // 2,) + value.shape)
    return lax.all_to_all(many, "col", 0, 0, axis_index_groups=groups)


def transposed(value):
    n_row, n_col = lax.axis_size("row"), lax.axis_size("col")
    pairs = []
    for r in range(n_row):
        for c in range(n_col):
            pairs.append((r * n_col + c, (c // 2) * n_col + r * 2 + c % 2))
    return lax.ppermute(value, ("row", "col"), pairs)


def mix_piece(plan, piece, top_piece, coef, third):
    moved = {0: piece, plan.top_bit: top_piece}
    far, far_value = plan.top_bit, plan.top
    if plan.col_far:
        pair = jnp.concatenate([piece, top_piece])
        pair = swap_far(pair, "col", third, plan.thirds, plan.col_blocks)
        moved[plan.third_bit] = pair[: piece.shape[0]]
        moved[plan.third_bit | plan.top_bit] = pair[piece.shape[0] :]
        far, far_value = far | plan.third_bit, far_value | plan.third
    mixed = []
    for j in range(plan.col_blocks):
        total = 0.0
        for m in range(plan.count):
            i = j ^ (plan.values[m] & ~far_value)
            source = moved[m & far][:, 128 * i : 128 * i + 128]
            total = total + source * coef[0, m, 8 + j][None, :]
        mixed.append(total)
    return jnp.concatenate(mixed, axis=1)


def mix_field(plan, covariance, over, coef, third):
    if not plan.col_far:
        return mix_near(plan, covariance, over, coef)
    if plan.row_far:
        mine, theirs = mix_rows(plan, covariance, over, coef)
        field = mine + swap_far(theirs, "row", third, plan.thirds, plan.row_blocks)
    else:
        (field,) = mix_rows(plan, covariance, over, coef)
    parts = [field, swap_far(field, "col", third, plan.thirds, plan.col_blocks)]
    return mix_cols(plan, parts, coef)


def shards(covariance, angles, delays, panel):
    rows_dev, cols_dev = covariance.shape
    n_row = lax.axis_size("row")
    row_blocks, col_blocks = rows_dev // QUANTUM, cols_dev // QUANTUM
    top = row_blocks * n_row // 2
    given = jnp.sum(delays) // QUANTUM - top - 1
    thirds = [1 << n for n in range(1, top.bit_length() - 1)]
    near = [t for t in thirds if t < min(row_blocks, col_blocks)]
    side = [t for t in thirds if col_blocks <= t < row_blocks]
    away = [t for t in thirds if t >= max(row_blocks, col_blocks)]
    plans = [Plan(group, top, row_blocks, col_blocks) for group in (near, side, away)]
    inner = (given > 1) & (given < top)
    third = jnp.where(inner, given, near[0])
    index = (third >= side[0]).astype(jnp.int32) + (third >= away[0]).astype(jnp.int32)
    rb = lax.axis_index("row").astype(jnp.int32) * row_blocks
    cb = lax.axis_index("col").astype(jnp.int32) * col_blocks
    info = jnp.concatenate([delays // QUANTUM, rb[None], cb[None], third[None]]).astype(jnp.int32)
    coef = coefficients(top, col_blocks, info, angles.reshape(3 * top, QUANTUM))

    sel_r = selection(coef, rb, row_blocks, 0, third, top, panel[0])
    sel_c = selection(coef, cb, col_blocks, 8, third, top, panel[0])
    part = jnp.dot(sel_r, covariance, precision=HIGHEST)
    covariance, part = lax.optimization_barrier((covariance, part))
    spread = lax.all_to_all(part.reshape(n_row, -1, cols_dev), "row", 0, 0)
    over = swap(covariance, "row", top // row_blocks)
    piece = jnp.sum(spread, axis=0)
    top_piece = swap(piece, "col", top // col_blocks)
    block = jnp.dot(piece, sel_c.T, precision=HIGHEST)
    block = block + swap(block, "col", 1)
    block = jnp.sum(gather_pairs(block), axis=0)
    over, block = lax.optimization_barrier((over, block))
    mixed = lax.switch(
        index, [functools.partial(mix_piece, plan) for plan in plans], piece, top_piece, coef, third
    )
    both = jnp.concatenate([mixed, block], axis=1)
    both = lax.all_to_all(jnp.broadcast_to(both[None], (n_row,) + both.shape), "row", 0, 0)
    mine, theirs = lax.switch(
        index, [functools.partial(mix_field, plan) for plan in plans], covariance, over, coef, third
    )
    theirs, both, mixed = lax.optimization_barrier((theirs, both, mixed))

    both = both.reshape(2 * PANEL, -1)
    rows_part, square = both[:, :cols_dev], both[:, cols_dev:]
    arrived = swap(theirs, "col", top // col_blocks)
    weights = solve_weights(square, rows_part)
    here = gather_pairs(transposed(mixed)).reshape(2 * PANEL, cols_dev)
    here, weights = lax.optimization_barrier((here, weights))
    twin = swap(here, "col", 1)
    low = lax.axis_index("col") % 2 == 0
    columns = jnp.concatenate([jnp.where(low, here, twin), jnp.where(low, twin, here)], axis=1)
    update = lax.dot_general(columns, weights, (((0,), (0,)), ((), ())), precision=HIGHEST)
    return mine + arrived - update


def solution(mesh):
    in_specs = (P("row", "col"), P(), P(), P())
    out_specs = P("row", "col")
    return jax.shard_map(shards, mesh=mesh, in_specs=in_specs, out_specs=out_specs, check_vma=False)
```

```python
import functools

import jax
import jax.numpy as jnp
from jax import lax
from jax.experimental import pallas as pl
from jax.experimental.pallas import tpu as pltpu
from jax.sharding import PartitionSpec as P

PANEL = 128
X, Y, Z_LO, Z_HI = 4, 4, 4, 4
QUANTUM = 128
HIGHEST = lax.Precision.HIGHEST
VMEM = pl.BlockSpec(memory_space=pltpu.VMEM)
SMEM = pl.BlockSpec(memory_space=pltpu.SMEM)


def swap(value, axis, mask):
    pairs = [(source, source ^ mask) for source in range(lax.axis_size(axis))]
    return lax.ppermute(value, axis, pairs)


def gather(value, axis, stride, count):
    size = lax.axis_size(axis)
    groups = [
        [low + stride * k + high for k in range(count)]
        for high in range(0, size, stride * count)
        for low in range(stride)
    ]
    many = jnp.broadcast_to(value[None], (count,) + value.shape)
    return lax.all_to_all(many, axis, 0, 0, axis_index_groups=groups)


def swap_far(value, axis, third, thirds, per_device):
    if len(thirds) == 1:
        return swap(value, axis, thirds[0] // per_device)
    index = sum((third > t).astype(jnp.int32) for t in thirds[:-1])
    ways = [functools.partial(swap, axis=axis, mask=t // per_device) for t in thirds]
    return lax.switch(index, ways, value)


class Plan:
    count, third_bit, top_bit = 8, 2, 4

    def __init__(self, thirds, top, row_blocks, col_blocks):
        third = thirds[0]
        self.third, self.thirds, self.top = third, thirds, top
        self.values = [(m & 1) + (m >> 1 & 1) * third + (m >> 2) * top for m in range(self.count)]
        self.row_blocks = row_blocks
        self.col_blocks = col_blocks
        self.row_far = third >= row_blocks
        self.col_far = third >= col_blocks


def coefficients_kernel(count, top, col_blocks, info, angles, out):
    gens = (1, info[5], top)
    rows = 16 * count
    rid = lax.broadcasted_iota(jnp.int32, (rows, top), 0)
    lane = lax.broadcasted_iota(jnp.int32, (rows, top), 1)
    slot = rid & 15
    base = jnp.where(slot < 8, info[3] + slot, info[4] + (slot & (col_blocks - 1)))
    mask = jnp.zeros_like(rid)
    for k, g in enumerate(gens):
        mask = mask | (((rid >> (4 + k)) & 1) * g)
    block = base ^ mask
    own, other, delays = [], [], []
    for section in range(3):
        d = info[section]
        source = (block & ~d) & (top - 1)
        pick = (source == lane).astype(jnp.float32)
        theta = angles[section * top : (section + 1) * top, :]
        low = (block[:, :1] & d) == 0
        cos = jnp.dot(pick, jnp.cos(theta), precision=HIGHEST, preferred_element_type=jnp.float32)
        sin = jnp.dot(pick, jnp.sin(theta), precision=HIGHEST, preferred_element_type=jnp.float32)
        sin = jnp.where(low, -sin, sin)
        own.append([cos[16 * m : 16 * m + 16] for m in range(count)])
        other.append([sin[16 * m : 16 * m + 16] for m in range(count)])
        delays.append(d)

    def partner(values, d, m):
        result = values[m ^ 1]
        for k, g in enumerate(gens[1:], 1):
            result = jnp.where(d == g, values[m ^ (1 << k)], result)
        return result

    one = jnp.ones((16, 128), jnp.float32)
    zero = jnp.zeros((16, 128), jnp.float32)

    def row_of(start):
        values = [one if m == start else zero for m in range(count)]
        for section in (2, 1, 0):
            a, b, d = own[section], other[section], delays[section]
            scaled = [values[m] * b[m] for m in range(count)]
            values = [values[m] * a[m] + partner(scaled, d, m) for m in range(count)]
        return values

    def col_of():
        values = [one if m == 0 else zero for m in range(count)]
        for section in (0, 1, 2):
            a, b, d = own[section], other[section], delays[section]
            values = [values[m] * a[m] + b[m] * partner(values, d, m) for m in range(count)]
        return values

    for n, values in enumerate(
        (row_of(0), row_of(Plan.top_bit), col_of(), row_of(Plan.third_bit))
    ):
        for m in range(count):
            out[n, m] = values[m]


def coefficients(top, col_blocks, info, angles):
    return pl.pallas_call(
        functools.partial(coefficients_kernel, Plan.count, top, col_blocks),
        out_shape=jax.ShapeDtypeStruct((4, Plan.count, 16, 128), jnp.float32),
        in_specs=[SMEM, VMEM],
        out_specs=VMEM,
        compiler_params=pltpu.CompilerParams(vmem_limit_bytes=32 * 2**20),
    )(info, angles)


def row_kernel(plan, height, near_ref, top_ref, coef_ref, *outs, rows=slice(0, 8)):
    tables = [0, 3]
    blocks = height // 128
    far = plan.third_bit if plan.row_far else 0
    for which, out in enumerate(outs):
        table = tables[which]
        columns = [jnp.transpose(coef_ref[table, m, rows, :]) for m in range(plan.count)]
        for j in range(blocks):
            total = None
            for m in range(plan.count):
                if m & far:
                    continue
                ref = top_ref if m & plan.top_bit else near_ref
                value = plan.values[m] & ~plan.top
                i = j ^ value
                term = ref[128 * i : 128 * i + 128, :] * columns[m][:, j : j + 1]
                total = term if total is None else total + term
            out[128 * j : 128 * j + 128, :] = total


def mix_rows(plan, near, top, coef, width=128):
    height, all_width = near.shape
    n_out = 2 if plan.row_far else 1
    block = pl.BlockSpec((height, width), lambda i: (0, i))
    shape = jax.ShapeDtypeStruct(near.shape, jnp.float32)
    return pl.pallas_call(
        functools.partial(row_kernel, plan, height),
        grid=(all_width // width,),
        out_shape=[shape] * n_out,
        in_specs=[block, block, VMEM],
        out_specs=[block] * n_out,
        compiler_params=pltpu.CompilerParams(vmem_limit_bytes=48 * 2**20),
    )(near, top, coef)


def col_kernel(plan, *refs):
    if plan.col_far:
        near_ref, far_ref, coef_ref, mine, theirs = refs
    else:
        near_ref, coef_ref, mine, theirs = refs
        far_ref = None
    far = plan.third_bit if plan.col_far else 0
    for which, out in enumerate((mine, theirs)):
        for j in range(plan.col_blocks):
            total = None
            for m in range(plan.count):
                if m & plan.top_bit:
                    continue
                ref = far_ref if m & far else near_ref
                value = plan.values[m] & ~(plan.third if m & far else 0)
                i = j ^ value
                term = ref[:, 128 * i : 128 * i + 128] * coef_ref[which, m, 8 + j : 9 + j, :]
                total = term if total is None else total + term
            out[:, 128 * j : 128 * j + 128] = total


def mix_cols(plan, parts, coef, strip=128):
    height, width = parts[0].shape
    block = pl.BlockSpec((strip, width), lambda i: (i, 0))
    shape = jax.ShapeDtypeStruct((height, width), jnp.float32)
    return pl.pallas_call(
        functools.partial(col_kernel, plan),
        grid=(height // strip,),
        out_shape=[shape] * 2,
        in_specs=[block] * len(parts) + [VMEM],
        out_specs=[block] * 2,
        compiler_params=pltpu.CompilerParams(vmem_limit_bytes=48 * 2**20),
    )(*parts, coef)


def near_kernel(plan, near_ref, top_ref, coef_ref, mine, theirs, middle):
    blocks = near_ref.shape[0] // QUANTUM
    rows = pl.ds(pl.program_id(0) * blocks, blocks)
    row_kernel(plan, near_ref.shape[0], near_ref, top_ref, coef_ref, middle, rows=rows)
    col_kernel(plan, middle, coef_ref, mine, theirs)


def mix_near(plan, near, top, coef):
    height, width = near.shape
    block = pl.BlockSpec((height // 2, width), lambda i: (i, 0))
    shape = jax.ShapeDtypeStruct((height, width), jnp.float32)
    return pl.pallas_call(
        functools.partial(near_kernel, plan),
        grid=(2,),
        out_shape=[shape] * 2,
        in_specs=[block, block, pl.BlockSpec(coef.shape, lambda i: (0, 0, 0, 0))],
        out_specs=[block] * 2,
        scratch_shapes=[pltpu.VMEM((height // 2, width), jnp.float32)],
        compiler_params=pltpu.CompilerParams(vmem_limit_bytes=48 * 2**20),
    )(near, top, coef)


def dot(a, b, over=((1,), (0,))):
    return lax.dot_general(
        a, b, (over, ((), ())), precision=HIGHEST, preferred_element_type=jnp.float32
    )


def inverse_factor(block):
    n = block.shape[0]
    i = lax.broadcasted_iota(jnp.int32, (8, 2 * n), 0)
    lane = lax.broadcasted_iota(jnp.int32, (8, 2 * n), 1)
    unit = [jnp.where(lane == i + 8 * t + n, 1.0, 0.0) for t in range(n // 8)]
    wide = jnp.concatenate([block, jnp.zeros_like(block)], axis=1)
    tiles = [wide[8 * t : 8 * t + 8] + unit[t] for t in range(n // 8)]
    for j in range(n):
        first, r = divmod(j, 8)
        row = tiles[first][r : r + 1, :]
        scaled = row * (1.0 / row[:, j : j + 1])
        for t in range(first, n // 8):
            col = tiles[t][:, j : j + 1]
            if t == first:
                col = jnp.where(i[:, :1] > r, col, 0.0)
            tiles[t] = tiles[t] - col * scaled
    out = []
    for t in range(n // 8):
        pivot = jnp.sum(jnp.where(lane == i + 8 * t, tiles[t], 0.0), axis=1, keepdims=True)
        out.append(tiles[t][:, n:] * lax.rsqrt(pivot))
    return jnp.concatenate(out, axis=0)


def weights_kernel(square, given, out, work, right):
    size, n = square.shape[0], 64
    work[...] = square[...]
    right[...] = given[...]
    inverses = []
    for k in range(0, size, n):
        inverse = inverse_factor(work[k : k + n, k : k + n])
        inverses.append(inverse)
        mine = dot(inverse, right[k : k + n, :])
        right[k : k + n, :] = mine
        if k + n < size:
            below = dot(work[k + n :, k : k + n], inverse, ((1,), (1,)))
            work[k + n :, k : k + n] = below
            work[k + n :, k + n :] -= dot(below, below, ((1,), (1,)))
            right[k + n :, :] -= dot(below, mine)
    for k in range(size - n, -1, -n):
        rest = right[k : k + n, :]
        if k + n < size:
            rest = rest - dot(work[k + n :, k : k + n], out[k + n :, :], ((0,), (0,)))
        out[k : k + n, :] = dot(inverses[k // n], rest, ((0,), (0,)))


def solve_weights(square, given):
    return pl.pallas_call(
        weights_kernel,
        out_shape=jax.ShapeDtypeStruct(given.shape, jnp.float32),
        in_specs=[VMEM, VMEM],
        out_specs=VMEM,
        scratch_shapes=[
            pltpu.VMEM(square.shape, jnp.float32),
            pltpu.VMEM(given.shape, jnp.float32),
        ],
        compiler_params=pltpu.CompilerParams(vmem_limit_bytes=32 * 2**20),
    )(square, given)


def selection(coef, base, n_blocks, first, third, top, panel):
    n = n_blocks * QUANTUM
    ids = base * QUANTUM + jnp.arange(n, dtype=jnp.int32)
    slots = jnp.arange(2 * PANEL, dtype=jnp.int32)
    chosen = panel + jnp.where(slots < PANEL, slots, top * QUANTUM + slots - PANEL)
    result = jnp.zeros((2 * PANEL, n), jnp.float32)
    for m in range(Plan.count):
        at = ids ^ (((m & 1) + (m >> 1 & 1) * third + (m >> 2) * top) * QUANTUM)
        weight = coef[2, m, first : first + n_blocks].reshape(n)
        result = result + jnp.where(at[None, :] == chosen[:, None], weight[None, :], 0.0)
    return result


def transposed(value):
    n_row, n_col = lax.axis_size("row"), lax.axis_size("col")
    cores = n_col // (Z_HI * Y)
    pairs = []
    for r in range(n_row):
        x, z_lo = divmod(r, Z_LO)
        for c in range(n_col):
            z_hi, y, core = c // cores // Y, c // cores % Y, c % cores
            to = (z_hi * Z_LO + y) * n_col + (z_lo * Y + x) * cores + core
            pairs.append((r * n_col + c, to))
    return lax.ppermute(value, ("row", "col"), pairs)


def mix_piece(plan, piece, top_piece, coef, third):
    moved = {0: piece, plan.top_bit: top_piece}
    far, far_value = plan.top_bit, plan.top
    if plan.col_far:
        pair = jnp.concatenate([piece, top_piece])
        pair = swap_far(pair, "col", third, plan.thirds, plan.col_blocks)
        moved[plan.third_bit] = pair[: piece.shape[0]]
        moved[plan.third_bit | plan.top_bit] = pair[piece.shape[0] :]
        far, far_value = far | plan.third_bit, far_value | plan.third
    mixed = []
    for j in range(plan.col_blocks):
        total = 0.0
        for m in range(plan.count):
            i = j ^ (plan.values[m] & ~far_value)
            source = moved[m & far][:, 128 * i : 128 * i + 128]
            total = total + source * coef[0, m, 8 + j][None, :]
        mixed.append(total)
    return jnp.concatenate(mixed, axis=1)


def mix_field(plan, covariance, over, coef, third):
    if not plan.col_far:
        return mix_near(plan, covariance, over, coef)
    if plan.row_far:
        mine, theirs = mix_rows(plan, covariance, over, coef)
        field = mine + swap_far(theirs, "row", third, plan.thirds, plan.row_blocks)
    else:
        (field,) = mix_rows(plan, covariance, over, coef)
    parts = [field, swap_far(field, "col", third, plan.thirds, plan.col_blocks)]
    return mix_cols(plan, parts, coef)


def shards(covariance, angles, delays, panel):
    rows_dev, cols_dev = covariance.shape
    n_row = lax.axis_size("row")
    row_blocks, col_blocks = rows_dev // QUANTUM, cols_dev // QUANTUM
    top = row_blocks * n_row // 2
    given = jnp.sum(delays) // QUANTUM - top - 1
    thirds = [1 << n for n in range(1, top.bit_length() - 1)]
    near = [t for t in thirds if t < min(row_blocks, col_blocks)]
    side = [t for t in thirds if col_blocks <= t < row_blocks]
    away = [t for t in thirds if t >= max(row_blocks, col_blocks)]
    plans = [Plan(group, top, row_blocks, col_blocks) for group in (near, side, away)]
    inner = (given > 1) & (given < top)
    third = jnp.where(inner, given, near[0])
    index = (third >= side[0]).astype(jnp.int32) + (third >= away[0]).astype(jnp.int32)
    rb = lax.axis_index("row").astype(jnp.int32) * row_blocks
    cb = lax.axis_index("col").astype(jnp.int32) * col_blocks
    info = jnp.concatenate([delays // QUANTUM, rb[None], cb[None], third[None]]).astype(jnp.int32)
    coef = coefficients(top, col_blocks, info, angles.reshape(3 * top, QUANTUM))

    sel_r = selection(coef, rb, row_blocks, 0, third, top, panel[0])
    sel_c = selection(coef, cb, col_blocks, 8, third, top, panel[0])
    part = jnp.dot(sel_r, covariance, precision=HIGHEST)
    spread = lax.all_to_all(part.reshape(n_row, -1, cols_dev), "row", 0, 0)
    over = swap(covariance, "row", top // row_blocks)
    piece = jnp.sum(spread, axis=0)
    block = jnp.dot(piece, sel_c.T, precision=HIGHEST)
    cores = lax.axis_size("col") // (Z_HI * Y)
    along = gather(jnp.concatenate([piece, block], axis=1), "col", cores * Y, Z_HI)
    z_hi = lax.axis_index("col") // (cores * Y)
    apart = top // col_blocks // (cores * Y)
    top_piece = lax.dynamic_index_in_dim(along, z_hi ^ apart, 0, keepdims=False)[:, :cols_dev]
    block = jnp.sum(along[:, :, cols_dev:], axis=0)
    mixed = lax.switch(
        index, [functools.partial(mix_piece, plan) for plan in plans], piece, top_piece, coef, third
    )
    quarter = gather(jnp.concatenate([mixed, block], axis=1), "row", 1, Z_LO)
    over, quarter = lax.optimization_barrier((over, quarter))
    quarter = quarter.reshape(-1, cols_dev + 2 * PANEL)
    flipped = transposed(quarter[:, :cols_dev])
    mine, moving = lax.switch(
        index,
        [functools.partial(mix_field, plan) for plan in plans],
        covariance, over, coef, third,
    )
    moving, quarter, flipped = lax.optimization_barrier((moving, quarter, flipped))

    arrived = swap(moving, "col", top // col_blocks)

    def finish(quarter, flipped, mine):
        pieces = jnp.concatenate([quarter[:, cols_dev:], flipped], axis=1)
        pieces = gather(pieces, "col", cores, Y)
        block = jnp.sum(pieces[:, :, : 2 * PANEL], axis=0)
        block = block + swap(block, "col", 1)
        here = pieces[:, :, 2 * PANEL :].reshape(2 * PANEL, cols_dev)
        twin = swap(here, "col", 1)
        both = gather(jnp.concatenate([quarter[:, :cols_dev], block], axis=1), "row", Z_LO, X)
        both = both.reshape(2 * PANEL, -1)
        weights = solve_weights(both[:, cols_dev:], both[:, :cols_dev])
        low = lax.axis_index("col") % 2 == 0
        columns = jnp.concatenate([jnp.where(low, here, twin), jnp.where(low, twin, here)], axis=1)
        update = lax.dot_general(columns, weights, (((0,), (0,)), ((), ())), precision=HIGHEST)
        return mine - update

    rest = lax.cond(
        panel[0] >= 0, finish, lambda quarter, flipped, mine: mine,
        quarter, flipped, mine,
    )
    return rest + arrived


def solution(mesh):
    in_specs = (P("row", "col"), P(), P(), P())
    out_specs = P("row", "col")
    return jax.shard_map(shards, mesh=mesh, in_specs=in_specs, out_specs=out_specs, check_vma=False)
```

```python
import functools

import jax
import jax.numpy as jnp
from jax import lax
from jax.experimental import pallas as pl
from jax.experimental.pallas import tpu as pltpu
from jax.sharding import PartitionSpec as P

PANEL = 128
X, Y, Z_LO, Z_HI = 4, 4, 4, 4
QUANTUM = 128
HIGHEST = lax.Precision.HIGHEST
VMEM = pl.BlockSpec(memory_space=pltpu.VMEM)
SMEM = pl.BlockSpec(memory_space=pltpu.SMEM)


def swap(value, axis, mask):
    pairs = [(source, source ^ mask) for source in range(lax.axis_size(axis))]
    return lax.ppermute(value, axis, pairs)


def z_hi_groups():
    size = lax.axis_size("col")
    rest = size // Z_HI
    return [list(range(low, size, rest)) for low in range(rest)]


def gather(value, axis, stride, count):
    size = lax.axis_size(axis)
    groups = [
        [low + stride * k + high for k in range(count)]
        for high in range(0, size, stride * count)
        for low in range(stride)
    ]
    many = jnp.broadcast_to(value[None], (count,) + value.shape)
    return lax.all_to_all(many, axis, 0, 0, axis_index_groups=groups)


def swap_far(value, axis, third, thirds, per_device):
    if len(thirds) == 1:
        return swap(value, axis, thirds[0] // per_device)
    index = sum((third > t).astype(jnp.int32) for t in thirds[:-1])
    ways = [functools.partial(swap, axis=axis, mask=t // per_device) for t in thirds]
    return lax.switch(index, ways, value)


class Plan:
    count, third_bit, top_bit = 8, 2, 4

    def __init__(self, thirds, top, row_blocks, col_blocks):
        third = thirds[0]
        self.third, self.thirds, self.top = third, thirds, top
        self.values = [(m & 1) + (m >> 1 & 1) * third + (m >> 2) * top for m in range(self.count)]
        self.row_blocks = row_blocks
        self.col_blocks = col_blocks
        self.row_far = third >= row_blocks
        self.col_far = third >= col_blocks


def coefficients_kernel(count, top, col_blocks, info, angles, out):
    gens = (1, info[5], top)
    rows = 16 * count
    rid = lax.broadcasted_iota(jnp.int32, (rows, top), 0)
    lane = lax.broadcasted_iota(jnp.int32, (rows, top), 1)
    slot = rid & 15
    base = jnp.where(slot < 8, info[3] + slot, info[4] + (slot & (col_blocks - 1)))
    mask = jnp.zeros_like(rid)
    for k, g in enumerate(gens):
        mask = mask | (((rid >> (4 + k)) & 1) * g)
    block = base ^ mask
    own, other, delays = [], [], []
    for section in range(3):
        d = info[section]
        source = (block & ~d) & (top - 1)
        pick = (source == lane).astype(jnp.float32)
        theta = angles[section * top : (section + 1) * top, :]
        low = (block[:, :1] & d) == 0
        cos = jnp.dot(pick, jnp.cos(theta), precision=HIGHEST, preferred_element_type=jnp.float32)
        sin = jnp.dot(pick, jnp.sin(theta), precision=HIGHEST, preferred_element_type=jnp.float32)
        sin = jnp.where(low, -sin, sin)
        own.append([cos[16 * m : 16 * m + 16] for m in range(count)])
        other.append([sin[16 * m : 16 * m + 16] for m in range(count)])
        delays.append(d)

    def partner(values, d, m):
        result = values[m ^ 1]
        for k, g in enumerate(gens[1:], 1):
            result = jnp.where(d == g, values[m ^ (1 << k)], result)
        return result

    one = jnp.ones((16, 128), jnp.float32)
    zero = jnp.zeros((16, 128), jnp.float32)

    def row_of(start):
        values = [one if m == start else zero for m in range(count)]
        for section in (2, 1, 0):
            a, b, d = own[section], other[section], delays[section]
            scaled = [values[m] * b[m] for m in range(count)]
            values = [values[m] * a[m] + partner(scaled, d, m) for m in range(count)]
        return values

    def col_of():
        values = [one if m == 0 else zero for m in range(count)]
        for section in (0, 1, 2):
            a, b, d = own[section], other[section], delays[section]
            values = [values[m] * a[m] + b[m] * partner(values, d, m) for m in range(count)]
        return values

    for n, values in enumerate(
        (row_of(0), row_of(Plan.top_bit), col_of(), row_of(Plan.third_bit),
         row_of(Plan.top_bit | Plan.third_bit))
    ):
        for m in range(count):
            out[n, m] = values[m]


def coefficients(top, col_blocks, info, angles):
    return pl.pallas_call(
        functools.partial(coefficients_kernel, Plan.count, top, col_blocks),
        out_shape=jax.ShapeDtypeStruct((5, Plan.count, 16, 128), jnp.float32),
        in_specs=[SMEM, VMEM],
        out_specs=VMEM,
        compiler_params=pltpu.CompilerParams(vmem_limit_bytes=32 * 2**20),
    )(info, angles)


def row_kernel(plan, height, near_ref, top_ref, coef_ref, *outs, rows=slice(0, 8)):
    tables = [0, 3]
    blocks = height // 128
    far = plan.third_bit if plan.row_far else 0
    for which, out in enumerate(outs):
        table = tables[which]
        columns = [jnp.transpose(coef_ref[table, m, rows, :]) for m in range(plan.count)]
        for j in range(blocks):
            total = None
            for m in range(plan.count):
                if m & far:
                    continue
                ref = top_ref if m & plan.top_bit else near_ref
                value = plan.values[m] & ~plan.top
                i = j ^ value
                term = ref[128 * i : 128 * i + 128, :] * columns[m][:, j : j + 1]
                total = term if total is None else total + term
            out[128 * j : 128 * j + 128, :] = total


def mix_rows(plan, near, top, coef, width=128):
    height, all_width = near.shape
    n_out = 2 if plan.row_far else 1
    block = pl.BlockSpec((height, width), lambda i: (0, i))
    shape = jax.ShapeDtypeStruct(near.shape, jnp.float32)
    return pl.pallas_call(
        functools.partial(row_kernel, plan, height),
        grid=(all_width // width,),
        out_shape=[shape] * n_out,
        in_specs=[block, block, VMEM],
        out_specs=[block] * n_out,
        compiler_params=pltpu.CompilerParams(vmem_limit_bytes=48 * 2**20),
    )(near, top, coef)


def col_kernel(plan, *refs):
    if plan.col_far:
        near_ref, far_ref, coef_ref, mine, theirs = refs
    else:
        near_ref, coef_ref, mine, theirs = refs
        far_ref = None
    far = plan.third_bit if plan.col_far else 0
    for which, out in enumerate((mine, theirs)):
        for j in range(plan.col_blocks):
            total = None
            for m in range(plan.count):
                if m & plan.top_bit:
                    continue
                ref = far_ref if m & far else near_ref
                value = plan.values[m] & ~(plan.third if m & far else 0)
                i = j ^ value
                term = ref[:, 128 * i : 128 * i + 128] * coef_ref[which, m, 8 + j : 9 + j, :]
                total = term if total is None else total + term
            out[:, 128 * j : 128 * j + 128] = total


def mix_cols(plan, parts, coef, strip=128):
    height, width = parts[0].shape
    block = pl.BlockSpec((strip, width), lambda i: (i, 0))
    shape = jax.ShapeDtypeStruct((height, width), jnp.float32)
    return pl.pallas_call(
        functools.partial(col_kernel, plan),
        grid=(height // strip,),
        out_shape=[shape] * 2,
        in_specs=[block] * len(parts) + [VMEM],
        out_specs=[block] * 2,
        compiler_params=pltpu.CompilerParams(vmem_limit_bytes=48 * 2**20),
    )(*parts, coef)


def deep_kernel(plan, place, field_ref, coef_ref, out_ref):
    tables = (0, 3, 1, 4)
    for to in range(4):
        for j in range(plan.col_blocks):
            total = None
            for m in range(plan.count):
                i = j ^ (m & 1)
                term = field_ref[place[0] ^ (m >> 1), :, 128 * i : 128 * i + 128]
                term = term * coef_ref[tables[to], m, 8 + j : 9 + j, :]
                total = term if total is None else total + term
            out_ref[place[0] ^ to, :, 128 * j : 128 * j + 128] = total


def mix_deep(plan, place, field, coef, strip=64):
    count, height, width = field.shape
    block = pl.BlockSpec((count, strip, width), lambda i: (0, i, 0))
    return pl.pallas_call(
        functools.partial(deep_kernel, plan),
        grid=(height // strip,),
        out_shape=jax.ShapeDtypeStruct(field.shape, jnp.float32),
        in_specs=[SMEM, block, VMEM],
        out_specs=block,
        compiler_params=pltpu.CompilerParams(vmem_limit_bytes=48 * 2**20),
    )(place, field, coef)


def near_kernel(plan, near_ref, top_ref, coef_ref, mine, theirs, middle):
    blocks = near_ref.shape[0] // QUANTUM
    rows = pl.ds(pl.program_id(0) * blocks, blocks)
    row_kernel(plan, near_ref.shape[0], near_ref, top_ref, coef_ref, middle, rows=rows)
    col_kernel(plan, middle, coef_ref, mine, theirs)


def mix_near(plan, near, top, coef):
    height, width = near.shape
    block = pl.BlockSpec((height // 2, width), lambda i: (i, 0))
    shape = jax.ShapeDtypeStruct((height, width), jnp.float32)
    return pl.pallas_call(
        functools.partial(near_kernel, plan),
        grid=(2,),
        out_shape=[shape] * 2,
        in_specs=[block, block, pl.BlockSpec(coef.shape, lambda i: (0, 0, 0, 0))],
        out_specs=[block] * 2,
        scratch_shapes=[pltpu.VMEM((height // 2, width), jnp.float32)],
        compiler_params=pltpu.CompilerParams(vmem_limit_bytes=48 * 2**20),
    )(near, top, coef)


def dot(a, b, over=((1,), (0,))):
    return lax.dot_general(
        a, b, (over, ((), ())), precision=HIGHEST, preferred_element_type=jnp.float32
    )


def inverse_factor(block):
    n = block.shape[0]
    i = lax.broadcasted_iota(jnp.int32, (8, 2 * n), 0)
    lane = lax.broadcasted_iota(jnp.int32, (8, 2 * n), 1)
    unit = [jnp.where(lane == i + 8 * t + n, 1.0, 0.0) for t in range(n // 8)]
    wide = jnp.concatenate([block, jnp.zeros_like(block)], axis=1)
    tiles = [wide[8 * t : 8 * t + 8] + unit[t] for t in range(n // 8)]
    for j in range(n):
        first, r = divmod(j, 8)
        row = tiles[first][r : r + 1, :]
        scaled = row * (1.0 / row[:, j : j + 1])
        for t in range(first, n // 8):
            col = tiles[t][:, j : j + 1]
            if t == first:
                col = jnp.where(i[:, :1] > r, col, 0.0)
            tiles[t] = tiles[t] - col * scaled
    out = []
    for t in range(n // 8):
        pivot = jnp.sum(jnp.where(lane == i + 8 * t, tiles[t], 0.0), axis=1, keepdims=True)
        out.append(tiles[t][:, n:] * lax.rsqrt(pivot))
    return jnp.concatenate(out, axis=0)


def weights_kernel(square, given, out, work, right):
    size, n = square.shape[0], 64
    work[...] = square[...]
    right[...] = given[...]
    inverses = []
    for k in range(0, size, n):
        inverse = inverse_factor(work[k : k + n, k : k + n])
        inverses.append(inverse)
        mine = dot(inverse, right[k : k + n, :])
        right[k : k + n, :] = mine
        if k + n < size:
            below = dot(work[k + n :, k : k + n], inverse, ((1,), (1,)))
            work[k + n :, k : k + n] = below
            work[k + n :, k + n :] -= dot(below, below, ((1,), (1,)))
            right[k + n :, :] -= dot(below, mine)
    for k in range(size - n, -1, -n):
        rest = right[k : k + n, :]
        if k + n < size:
            rest = rest - dot(work[k + n :, k : k + n], out[k + n :, :], ((0,), (0,)))
        out[k : k + n, :] = dot(inverses[k // n], rest, ((0,), (0,)))


def solve_weights(square, given):
    return pl.pallas_call(
        weights_kernel,
        out_shape=jax.ShapeDtypeStruct(given.shape, jnp.float32),
        in_specs=[VMEM, VMEM],
        out_specs=VMEM,
        scratch_shapes=[
            pltpu.VMEM(square.shape, jnp.float32),
            pltpu.VMEM(given.shape, jnp.float32),
        ],
        compiler_params=pltpu.CompilerParams(vmem_limit_bytes=32 * 2**20),
    )(square, given)


def selection(coef, base, n_blocks, first, third, top, panel):
    n = n_blocks * QUANTUM
    ids = base * QUANTUM + jnp.arange(n, dtype=jnp.int32)
    slots = jnp.arange(2 * PANEL, dtype=jnp.int32)
    chosen = panel + jnp.where(slots < PANEL, slots, top * QUANTUM + slots - PANEL)
    result = jnp.zeros((2 * PANEL, n), jnp.float32)
    for m in range(Plan.count):
        at = ids ^ (((m & 1) + (m >> 1 & 1) * third + (m >> 2) * top) * QUANTUM)
        weight = coef[2, m, first : first + n_blocks].reshape(n)
        result = result + jnp.where(at[None, :] == chosen[:, None], weight[None, :], 0.0)
    return result


def transposed(value):
    n_row, n_col = lax.axis_size("row"), lax.axis_size("col")
    cores = n_col // (Z_HI * Y)
    pairs = []
    for r in range(n_row):
        x, z_lo = divmod(r, Z_LO)
        for c in range(n_col):
            z_hi, y, core = c // cores // Y, c // cores % Y, c % cores
            to = (z_hi * Z_LO + y) * n_col + (z_lo * Y + x) * cores + core
            pairs.append((r * n_col + c, to))
    return lax.ppermute(value, ("row", "col"), pairs)


def mix_piece(plan, piece, top_piece, coef, third):
    moved = {0: piece, plan.top_bit: top_piece}
    far, far_value = plan.top_bit, plan.top
    if plan.col_far:
        pair = jnp.concatenate([piece, top_piece])
        pair = swap_far(pair, "col", third, plan.thirds, plan.col_blocks)
        moved[plan.third_bit] = pair[: piece.shape[0]]
        moved[plan.third_bit | plan.top_bit] = pair[piece.shape[0] :]
        far, far_value = far | plan.third_bit, far_value | plan.third
    mixed = []
    for j in range(plan.col_blocks):
        total = 0.0
        for m in range(plan.count):
            i = j ^ (plan.values[m] & ~far_value)
            source = moved[m & far][:, 128 * i : 128 * i + 128]
            total = total + source * coef[0, m, 8 + j][None, :]
        mixed.append(total)
    return jnp.concatenate(mixed, axis=1)


def mix_field(plan, covariance, over, coef, third):
    if not plan.col_far:
        return mix_near(plan, covariance, over, coef)
    if plan.row_far:
        mine, theirs = mix_rows(plan, covariance, over, coef)
        field = mine + swap_far(theirs, "row", third, plan.thirds, plan.row_blocks)
    else:
        (field,) = mix_rows(plan, covariance, over, coef)
    parts = [field, swap_far(field, "col", third, plan.thirds, plan.col_blocks)]
    return mix_cols(plan, parts, coef)


def shards(covariance, angles, delays, panel):
    rows_dev, cols_dev = covariance.shape
    n_row = lax.axis_size("row")
    row_blocks, col_blocks = rows_dev // QUANTUM, cols_dev // QUANTUM
    top = row_blocks * n_row // 2
    given = jnp.sum(delays) // QUANTUM - top - 1
    thirds = [1 << n for n in range(1, top.bit_length() - 1)]
    near = [t for t in thirds if t < min(row_blocks, col_blocks)]
    side = [t for t in thirds if col_blocks <= t < row_blocks]
    cores = lax.axis_size("col") // (Z_HI * Y)
    inner_z = col_blocks * cores * Y
    away = [t for t in thirds if max(row_blocks, col_blocks) <= t < inner_z]
    deep = [t for t in thirds if t >= inner_z]
    plans = [Plan(group, top, row_blocks, col_blocks) for group in (near, side, away, deep)]
    inner = (given > 1) & (given < top)
    third = jnp.where(inner, given, near[0])
    index = sum((third >= group[0]).astype(jnp.int32) for group in (side, away, deep))
    rb = lax.axis_index("row").astype(jnp.int32) * row_blocks
    cb = lax.axis_index("col").astype(jnp.int32) * col_blocks
    info = jnp.concatenate([delays // QUANTUM, rb[None], cb[None], third[None]]).astype(jnp.int32)
    coef = coefficients(top, col_blocks, info, angles.reshape(3 * top, QUANTUM))

    sel_r = selection(coef, rb, row_blocks, 0, third, top, panel[0])
    sel_c = selection(coef, cb, col_blocks, 8, third, top, panel[0])
    part = jnp.dot(sel_r, covariance, precision=HIGHEST)
    spread = lax.all_to_all(part.reshape(n_row, -1, cols_dev), "row", 0, 0)
    over = swap(covariance, "row", top // row_blocks)
    piece = jnp.sum(spread, axis=0)
    block = jnp.dot(piece, sel_c.T, precision=HIGHEST)
    along = gather(jnp.concatenate([piece, block], axis=1), "col", cores * Y, Z_HI)
    z_hi = lax.axis_index("col") // (cores * Y)
    apart = top // col_blocks // (cores * Y)
    top_piece = lax.dynamic_index_in_dim(along, z_hi ^ apart, 0, keepdims=False)[:, :cols_dev]
    block = jnp.sum(along[:, :, cols_dev:], axis=0)
    mixed = lax.switch(
        index, [functools.partial(mix_piece, plan) for plan in plans], piece, top_piece, coef, third
    )
    quarter = gather(jnp.concatenate([mixed, block], axis=1), "row", 1, Z_LO)
    over, quarter = lax.optimization_barrier((over, quarter))
    quarter = quarter.reshape(-1, cols_dev + 2 * PANEL)

    def finish(quarter, flipped, mine):
        pieces = jnp.concatenate([quarter[:, cols_dev:], flipped], axis=1)
        pieces = gather(pieces, "col", cores, Y)
        block = jnp.sum(pieces[:, :, : 2 * PANEL], axis=0)
        block = block + swap(block, "col", 1)
        here = pieces[:, :, 2 * PANEL :].reshape(2 * PANEL, cols_dev)
        twin = swap(here, "col", 1)
        both = gather(jnp.concatenate([quarter[:, :cols_dev], block], axis=1), "row", Z_LO, X)
        both = both.reshape(2 * PANEL, -1)
        weights = solve_weights(both[:, cols_dev:], both[:, :cols_dev])
        low = lax.axis_index("col") % 2 == 0
        columns = jnp.concatenate([jnp.where(low, here, twin), jnp.where(low, twin, here)], axis=1)
        update = lax.dot_general(columns, weights, (((0,), (0,)), ((), ())), precision=HIGHEST)
        return mine - update

    def close(quarter, flipped, mine):
        return lax.cond(
            panel[0] >= 0, finish, lambda quarter, flipped, mine: mine, quarter, flipped, mine
        )

    def plain(covariance, over, quarter, coef):
        flipped = transposed(quarter[:, :cols_dev])
        mine, moving = lax.switch(
            index,
            [functools.partial(mix_field, plan) for plan in plans[:3]],
            covariance, over, coef, third,
        )
        arrived = swap(moving, "col", top // col_blocks)
        return close(quarter, flipped, mine) + arrived

    def through(covariance, over, quarter, coef):
        plan = plans[3]
        flipped = transposed(quarter[:, :cols_dev])
        mine, theirs = mix_rows(plan, covariance, over, coef)
        field = mine + swap(theirs, "row", plan.third // row_blocks)
        field, flipped = lax.optimization_barrier((field, flipped))
        field = field.reshape(Z_HI, -1, cols_dev)
        field = lax.all_to_all(field, "col", 0, 0, axis_index_groups=z_hi_groups())
        field = mix_deep(plan, z_hi.astype(jnp.int32)[None], field, coef)
        field, quarter, flipped = lax.optimization_barrier((field, quarter, flipped))
        parts = [lax.dynamic_index_in_dim(field, z_hi ^ k) for k in range(Z_HI)]
        parts[1:] = [swap(parts[k], "col", k * cores * Y) for k in range(1, Z_HI)]
        rest = close(quarter, flipped, jnp.zeros((rows_dev, cols_dev), jnp.float32))
        for k, part in enumerate(parts):
            field = lax.dynamic_update_slice(field, part, (z_hi ^ k, 0, 0))
        return rest + field.reshape(rows_dev, cols_dev)

    return lax.cond(index == 3, through, plain, covariance, over, quarter, coef)


def solution(mesh):
    in_specs = (P("row", "col"), P(), P(), P())
    out_specs = P("row", "col")
    return jax.shard_map(shards, mesh=mesh, in_specs=in_specs, out_specs=out_specs, check_vma=False)
```

```python
import functools

import jax
import jax.numpy as jnp
from jax import lax
from jax.experimental import pallas as pl
from jax.experimental.pallas import tpu as pltpu
from jax.sharding import PartitionSpec as P

PANEL = 128
X, Y, Z_LO, Z_HI = 4, 4, 4, 4
QUANTUM = 128
HIGHEST = lax.Precision.HIGHEST
VMEM = pl.BlockSpec(memory_space=pltpu.VMEM)
SMEM = pl.BlockSpec(memory_space=pltpu.SMEM)


def swap(value, axis, mask):
    pairs = [(source, source ^ mask) for source in range(lax.axis_size(axis))]
    return lax.ppermute(value, axis, pairs)


def z_hi_groups():
    size = lax.axis_size("col")
    rest = size // Z_HI
    return [list(range(low, size, rest)) for low in range(rest)]


def gather(value, axis, stride, count):
    size = lax.axis_size(axis)
    groups = [
        [low + stride * k + high for k in range(count)]
        for high in range(0, size, stride * count)
        for low in range(stride)
    ]
    many = jnp.broadcast_to(value[None], (count,) + value.shape)
    return lax.all_to_all(many, axis, 0, 0, axis_index_groups=groups)


def swap_far(value, axis, third, thirds, per_device):
    if len(thirds) == 1:
        return swap(value, axis, thirds[0] // per_device)
    index = sum((third > t).astype(jnp.int32) for t in thirds[:-1])
    ways = [functools.partial(swap, axis=axis, mask=t // per_device) for t in thirds]
    return lax.switch(index, ways, value)


class Plan:
    count, third_bit, top_bit = 8, 2, 4

    def __init__(self, thirds, top, row_blocks, col_blocks):
        third = thirds[0]
        self.third, self.thirds, self.top = third, thirds, top
        self.values = [(m & 1) + (m >> 1 & 1) * third + (m >> 2) * top for m in range(self.count)]
        self.row_blocks = row_blocks
        self.col_blocks = col_blocks
        self.row_far = third >= row_blocks
        self.col_far = third >= col_blocks


def coefficients_kernel(count, top, col_blocks, info, angles, out):
    gens = (1, info[5], top)
    rows = 16 * count
    rid = lax.broadcasted_iota(jnp.int32, (rows, top), 0)
    lane = lax.broadcasted_iota(jnp.int32, (rows, top), 1)
    slot = rid & 15
    base = jnp.where(slot < 8, info[3] + slot, info[4] + (slot & (col_blocks - 1)))
    mask = jnp.zeros_like(rid)
    for k, g in enumerate(gens):
        mask = mask | (((rid >> (4 + k)) & 1) * g)
    block = base ^ mask
    own, other, delays = [], [], []
    for section in range(3):
        d = info[section]
        source = (block & ~d) & (top - 1)
        pick = (source == lane).astype(jnp.float32)
        theta = angles[section * top : (section + 1) * top, :]
        low = (block[:, :1] & d) == 0
        cos = jnp.dot(pick, jnp.cos(theta), precision=HIGHEST, preferred_element_type=jnp.float32)
        sin = jnp.dot(pick, jnp.sin(theta), precision=HIGHEST, preferred_element_type=jnp.float32)
        sin = jnp.where(low, -sin, sin)
        own.append([cos[16 * m : 16 * m + 16] for m in range(count)])
        other.append([sin[16 * m : 16 * m + 16] for m in range(count)])
        delays.append(d)

    def partner(values, d, m):
        result = values[m ^ 1]
        for k, g in enumerate(gens[1:], 1):
            result = jnp.where(d == g, values[m ^ (1 << k)], result)
        return result

    one = jnp.ones((16, 128), jnp.float32)
    zero = jnp.zeros((16, 128), jnp.float32)

    def row_of(start):
        values = [one if m == start else zero for m in range(count)]
        for section in (2, 1, 0):
            a, b, d = own[section], other[section], delays[section]
            scaled = [values[m] * b[m] for m in range(count)]
            values = [values[m] * a[m] + partner(scaled, d, m) for m in range(count)]
        return values

    def col_of():
        values = [one if m == 0 else zero for m in range(count)]
        for section in (0, 1, 2):
            a, b, d = own[section], other[section], delays[section]
            values = [values[m] * a[m] + b[m] * partner(values, d, m) for m in range(count)]
        return values

    for n, values in enumerate(
        (row_of(0), row_of(Plan.top_bit), col_of(), row_of(Plan.third_bit),
         row_of(Plan.top_bit | Plan.third_bit))
    ):
        for m in range(count):
            out[n, m] = values[m]


def coefficients(top, col_blocks, info, angles):
    return pl.pallas_call(
        functools.partial(coefficients_kernel, Plan.count, top, col_blocks),
        out_shape=jax.ShapeDtypeStruct((5, Plan.count, 16, 128), jnp.float32),
        in_specs=[SMEM, VMEM],
        out_specs=VMEM,
        compiler_params=pltpu.CompilerParams(vmem_limit_bytes=32 * 2**20),
    )(info, angles)


def row_kernel(plan, height, near_ref, top_ref, coef_ref, *outs, rows=slice(0, 8)):
    tables = [0, 3]
    blocks = height // 128
    far = plan.third_bit if plan.row_far else 0
    for which, out in enumerate(outs):
        table = tables[which]
        columns = [jnp.transpose(coef_ref[table, m, rows, :]) for m in range(plan.count)]
        for j in range(blocks):
            total = None
            for m in range(plan.count):
                if m & far:
                    continue
                ref = top_ref if m & plan.top_bit else near_ref
                value = plan.values[m] & ~plan.top
                i = j ^ value
                term = ref[128 * i : 128 * i + 128, :] * columns[m][:, j : j + 1]
                total = term if total is None else total + term
            out[128 * j : 128 * j + 128, :] = total


def mix_rows(plan, near, top, coef, width=128):
    height, all_width = near.shape
    n_out = 2 if plan.row_far else 1
    block = pl.BlockSpec((height, width), lambda i: (0, i))
    shape = jax.ShapeDtypeStruct(near.shape, jnp.float32)
    return pl.pallas_call(
        functools.partial(row_kernel, plan, height),
        grid=(all_width // width,),
        out_shape=[shape] * n_out,
        in_specs=[block, block, VMEM],
        out_specs=[block] * n_out,
        compiler_params=pltpu.CompilerParams(vmem_limit_bytes=48 * 2**20),
    )(near, top, coef)


def col_kernel(plan, *refs):
    if plan.col_far:
        near_ref, far_ref, coef_ref, mine, theirs = refs
    else:
        near_ref, coef_ref, mine, theirs = refs
        far_ref = None
    far = plan.third_bit if plan.col_far else 0
    for which, out in enumerate((mine, theirs)):
        for j in range(plan.col_blocks):
            total = None
            for m in range(plan.count):
                if m & plan.top_bit:
                    continue
                ref = far_ref if m & far else near_ref
                value = plan.values[m] & ~(plan.third if m & far else 0)
                i = j ^ value
                term = ref[:, 128 * i : 128 * i + 128] * coef_ref[which, m, 8 + j : 9 + j, :]
                total = term if total is None else total + term
            out[:, 128 * j : 128 * j + 128] = total


def mix_cols(plan, parts, coef, strip=128):
    height, width = parts[0].shape
    block = pl.BlockSpec((strip, width), lambda i: (i, 0))
    shape = jax.ShapeDtypeStruct((height, width), jnp.float32)
    return pl.pallas_call(
        functools.partial(col_kernel, plan),
        grid=(height // strip,),
        out_shape=[shape] * 2,
        in_specs=[block] * len(parts) + [VMEM],
        out_specs=[block] * 2,
        compiler_params=pltpu.CompilerParams(vmem_limit_bytes=48 * 2**20),
    )(*parts, coef)


def deep_kernel(plan, place, field_ref, coef_ref, out_ref):
    tables = (0, 3, 1, 4)
    for to in range(4):
        for j in range(plan.col_blocks):
            total = None
            for m in range(plan.count):
                i = j ^ (m & 1)
                term = field_ref[place[0] ^ (m >> 1), :, 128 * i : 128 * i + 128]
                term = term * coef_ref[tables[to], m, 8 + j : 9 + j, :]
                total = term if total is None else total + term
            out_ref[place[0] ^ to, :, 128 * j : 128 * j + 128] = total


def mix_deep(plan, place, field, coef, strip=64):
    count, height, width = field.shape
    block = pl.BlockSpec((count, strip, width), lambda i: (0, i, 0))
    return pl.pallas_call(
        functools.partial(deep_kernel, plan),
        grid=(height // strip,),
        out_shape=jax.ShapeDtypeStruct(field.shape, jnp.float32),
        in_specs=[SMEM, block, VMEM],
        out_specs=block,
        compiler_params=pltpu.CompilerParams(vmem_limit_bytes=48 * 2**20),
    )(place, field, coef)


def near_kernel(plan, near_ref, top_ref, coef_ref, mine, theirs, middle):
    blocks = near_ref.shape[0] // QUANTUM
    rows = pl.ds(pl.program_id(0) * blocks, blocks)
    row_kernel(plan, near_ref.shape[0], near_ref, top_ref, coef_ref, middle, rows=rows)
    col_kernel(plan, middle, coef_ref, mine, theirs)


def mix_near(plan, near, top, coef):
    height, width = near.shape
    block = pl.BlockSpec((height // 2, width), lambda i: (i, 0))
    shape = jax.ShapeDtypeStruct((height, width), jnp.float32)
    return pl.pallas_call(
        functools.partial(near_kernel, plan),
        grid=(2,),
        out_shape=[shape] * 2,
        in_specs=[block, block, pl.BlockSpec(coef.shape, lambda i: (0, 0, 0, 0))],
        out_specs=[block] * 2,
        scratch_shapes=[pltpu.VMEM((height // 2, width), jnp.float32)],
        compiler_params=pltpu.CompilerParams(vmem_limit_bytes=48 * 2**20),
    )(near, top, coef)


def dot(a, b, over=((1,), (0,))):
    return lax.dot_general(
        a, b, (over, ((), ())), precision=HIGHEST, preferred_element_type=jnp.float32
    )


def inverse_factor(block):
    n = block.shape[0]
    i = lax.broadcasted_iota(jnp.int32, (8, 2 * n), 0)
    lane = lax.broadcasted_iota(jnp.int32, (8, 2 * n), 1)
    unit = [jnp.where(lane == i + 8 * t + n, 1.0, 0.0) for t in range(n // 8)]
    wide = jnp.concatenate([block, jnp.zeros_like(block)], axis=1)
    tiles = [wide[8 * t : 8 * t + 8] + unit[t] for t in range(n // 8)]
    for j in range(n):
        first, r = divmod(j, 8)
        row = tiles[first][r : r + 1, :]
        scaled = row * (1.0 / row[:, j : j + 1])
        for t in range(first, n // 8):
            col = tiles[t][:, j : j + 1]
            if t == first:
                col = jnp.where(i[:, :1] > r, col, 0.0)
            tiles[t] = tiles[t] - col * scaled
    out = []
    for t in range(n // 8):
        pivot = jnp.sum(jnp.where(lane == i + 8 * t, tiles[t], 0.0), axis=1, keepdims=True)
        out.append(tiles[t][:, n:] * lax.rsqrt(pivot))
    return jnp.concatenate(out, axis=0)


def weights_kernel(square, given, out, work, right):
    size, n = square.shape[0], 64
    work[...] = square[...]
    right[...] = given[...]
    inverses = []
    for k in range(0, size, n):
        inverse = inverse_factor(work[k : k + n, k : k + n])
        inverses.append(inverse)
        mine = dot(inverse, right[k : k + n, :])
        right[k : k + n, :] = mine
        if k + n < size:
            below = dot(work[k + n :, k : k + n], inverse, ((1,), (1,)))
            work[k + n :, k : k + n] = below
            work[k + n :, k + n :] -= dot(below, below, ((1,), (1,)))
            right[k + n :, :] -= dot(below, mine)
    for k in range(size - n, -1, -n):
        rest = right[k : k + n, :]
        if k + n < size:
            rest = rest - dot(work[k + n :, k : k + n], out[k + n :, :], ((0,), (0,)))
        out[k : k + n, :] = dot(inverses[k // n], rest, ((0,), (0,)))


def solve_weights(square, given):
    return pl.pallas_call(
        weights_kernel,
        out_shape=jax.ShapeDtypeStruct(given.shape, jnp.float32),
        in_specs=[VMEM, VMEM],
        out_specs=VMEM,
        scratch_shapes=[
            pltpu.VMEM(square.shape, jnp.float32),
            pltpu.VMEM(given.shape, jnp.float32),
        ],
        compiler_params=pltpu.CompilerParams(vmem_limit_bytes=32 * 2**20),
    )(square, given)


def selection(coef, base, n_blocks, first, third, top, panel):
    n = n_blocks * QUANTUM
    ids = base * QUANTUM + jnp.arange(n, dtype=jnp.int32)
    slots = jnp.arange(2 * PANEL, dtype=jnp.int32)
    chosen = panel + jnp.where(slots < PANEL, slots, top * QUANTUM + slots - PANEL)
    result = jnp.zeros((2 * PANEL, n), jnp.float32)
    for m in range(Plan.count):
        at = ids ^ (((m & 1) + (m >> 1 & 1) * third + (m >> 2) * top) * QUANTUM)
        weight = coef[2, m, first : first + n_blocks].reshape(n)
        result = result + jnp.where(at[None, :] == chosen[:, None], weight[None, :], 0.0)
    return result


def transposed(value):
    n_row, n_col = lax.axis_size("row"), lax.axis_size("col")
    cores = n_col // (Z_HI * Y)
    pairs = []
    for r in range(n_row):
        x, z_lo = divmod(r, Z_LO)
        for c in range(n_col):
            z_hi, y, core = c // cores // Y, c // cores % Y, c % cores
            to = (z_hi * Z_LO + y) * n_col + (z_lo * Y + x) * cores + core
            pairs.append((r * n_col + c, to))
    return lax.ppermute(value, ("row", "col"), pairs)


def mix_piece(plan, piece, top_piece, coef, third):
    moved = {0: piece, plan.top_bit: top_piece}
    far, far_value = plan.top_bit, plan.top
    if plan.col_far:
        pair = jnp.concatenate([piece, top_piece])
        pair = swap_far(pair, "col", third, plan.thirds, plan.col_blocks)
        moved[plan.third_bit] = pair[: piece.shape[0]]
        moved[plan.third_bit | plan.top_bit] = pair[piece.shape[0] :]
        far, far_value = far | plan.third_bit, far_value | plan.third
    mixed = []
    for j in range(plan.col_blocks):
        total = 0.0
        for m in range(plan.count):
            i = j ^ (plan.values[m] & ~far_value)
            source = moved[m & far][:, 128 * i : 128 * i + 128]
            total = total + source * coef[0, m, 8 + j][None, :]
        mixed.append(total)
    return jnp.concatenate(mixed, axis=1)


def mix_field(plan, covariance, over, coef, third):
    if not plan.col_far:
        return mix_near(plan, covariance, over, coef)
    if plan.row_far:
        mine, theirs = mix_rows(plan, covariance, over, coef)
        field = mine + swap_far(theirs, "row", third, plan.thirds, plan.row_blocks)
    else:
        (field,) = mix_rows(plan, covariance, over, coef)
    parts = [field, swap_far(field, "col", third, plan.thirds, plan.col_blocks)]
    return mix_cols(plan, parts, coef)


def shards(covariance, angles, delays, panel):
    rows_dev, cols_dev = covariance.shape
    n_row = lax.axis_size("row")
    row_blocks, col_blocks = rows_dev // QUANTUM, cols_dev // QUANTUM
    top = row_blocks * n_row // 2
    given = jnp.sum(delays) // QUANTUM - top - 1
    thirds = [1 << n for n in range(1, top.bit_length() - 1)]
    near = [t for t in thirds if t < min(row_blocks, col_blocks)]
    side = [t for t in thirds if col_blocks <= t < row_blocks]
    cores = lax.axis_size("col") // (Z_HI * Y)
    inner_z = col_blocks * cores * Y
    away = [t for t in thirds if max(row_blocks, col_blocks) <= t < inner_z]
    deep = [t for t in thirds if t >= inner_z]
    plans = [Plan(group, top, row_blocks, col_blocks) for group in (near, side, away, deep)]
    inner = (given > 1) & (given < top)
    third = jnp.where(inner, given, near[0])
    index = sum((third >= group[0]).astype(jnp.int32) for group in (side, away, deep))
    rb = lax.axis_index("row").astype(jnp.int32) * row_blocks
    cb = lax.axis_index("col").astype(jnp.int32) * col_blocks
    info = jnp.concatenate([delays // QUANTUM, rb[None], cb[None], third[None]]).astype(jnp.int32)
    coef = coefficients(top, col_blocks, info, angles.reshape(3 * top, QUANTUM))

    sel_r = selection(coef, rb, row_blocks, 0, third, top, panel[0])
    sel_c = selection(coef, cb, col_blocks, 8, third, top, panel[0])
    part = jnp.dot(sel_r, covariance, precision=HIGHEST)
    spread = lax.all_to_all(part.reshape(n_row, -1, cols_dev), "row", 0, 0)
    over = swap(covariance, "row", top // row_blocks)
    piece = jnp.sum(spread, axis=0)
    block = jnp.dot(piece, sel_c.T, precision=HIGHEST)
    along = gather(jnp.concatenate([piece, block], axis=1), "col", cores * Y, Z_HI)
    z_hi = lax.axis_index("col") // (cores * Y)
    apart = top // col_blocks // (cores * Y)
    top_piece = lax.dynamic_index_in_dim(along, z_hi ^ apart, 0, keepdims=False)[:, :cols_dev]
    block = jnp.sum(along[:, :, cols_dev:], axis=0)
    mixed = lax.switch(
        index, [functools.partial(mix_piece, plan) for plan in plans], piece, top_piece, coef, third
    )
    quarter = gather(jnp.concatenate([mixed, block], axis=1), "row", 1, Z_LO)
    quarter = quarter.reshape(-1, cols_dev + 2 * PANEL)
    flipped = transposed(quarter[:, :cols_dev])
    over, quarter, flipped = lax.optimization_barrier((over, quarter, flipped))

    def finish(quarter, flipped):
        pieces = jnp.concatenate([quarter[:, cols_dev:], flipped], axis=1)
        pieces = gather(pieces, "col", cores, Y)
        block = jnp.sum(pieces[:, :, : 2 * PANEL], axis=0)
        block = block + swap(block, "col", 1)
        here = pieces[:, :, 2 * PANEL :].reshape(2 * PANEL, cols_dev)
        twin = swap(here, "col", 1)
        both = gather(jnp.concatenate([quarter[:, :cols_dev], block], axis=1), "row", Z_LO, X)
        both = both.reshape(2 * PANEL, -1)
        weights = solve_weights(both[:, cols_dev:], both[:, :cols_dev])
        low = lax.axis_index("col") % 2 == 0
        columns = jnp.concatenate([jnp.where(low, here, twin), jnp.where(low, twin, here)], axis=1)
        return lax.dot_general(columns, weights, (((0,), (0,)), ((), ())), precision=HIGHEST)

    def close(quarter, flipped):
        def skip(quarter, flipped):
            return jnp.zeros((rows_dev, cols_dev), jnp.float32)

        return lax.cond(panel[0] >= 0, finish, skip, quarter, flipped)

    def plain(covariance, over, quarter, flipped, coef):
        mine, moving = lax.switch(
            index,
            [functools.partial(mix_field, plan) for plan in plans[:3]],
            covariance, over, coef, third,
        )
        arrived = swap(moving, "col", top // col_blocks)
        return mine + arrived - close(quarter, flipped)

    def through(covariance, over, quarter, flipped, coef):
        plan = plans[3]
        mine, theirs = mix_rows(plan, covariance, over, coef)
        field = mine + swap(theirs, "row", plan.third // row_blocks)
        field = field.reshape(Z_HI, -1, cols_dev)
        field = lax.all_to_all(field, "col", 0, 0, axis_index_groups=z_hi_groups())
        field = mix_deep(plan, z_hi.astype(jnp.int32)[None], field, coef)
        parts = [lax.dynamic_index_in_dim(field, z_hi ^ k) for k in range(Z_HI)]
        parts[1:] = [swap(parts[k], "col", k * cores * Y) for k in range(1, Z_HI)]
        update = close(quarter, flipped)
        for k, part in enumerate(parts):
            field = lax.dynamic_update_slice(field, part, (z_hi ^ k, 0, 0))
        return field.reshape(rows_dev, cols_dev) - update

    return lax.cond(index == 3, through, plain, covariance, over, quarter, flipped, coef)


def solution(mesh):
    in_specs = (P("row", "col"), P(), P(), P())
    out_specs = P("row", "col")
    return jax.shard_map(shards, mesh=mesh, in_specs=in_specs, out_specs=out_specs, check_vma=False)
```

```python
import functools

import jax
import jax.numpy as jnp
from jax import lax
from jax.experimental import pallas as pl
from jax.experimental.pallas import tpu as pltpu
from jax.sharding import PartitionSpec as P

PANEL = 128
X, Y, Z_LO, Z_HI = 4, 4, 4, 4
QUANTUM = 128
HIGHEST = lax.Precision.HIGHEST
VMEM = pl.BlockSpec(memory_space=pltpu.VMEM)
SMEM = pl.BlockSpec(memory_space=pltpu.SMEM)


def swap(value, axis, mask):
    pairs = [(source, source ^ mask) for source in range(lax.axis_size(axis))]
    return lax.ppermute(value, axis, pairs)


def gather(value, axis, stride, count):
    size = lax.axis_size(axis)
    groups = [
        [low + stride * k + high for k in range(count)]
        for high in range(0, size, stride * count)
        for low in range(stride)
    ]
    many = jnp.broadcast_to(value[None], (count,) + value.shape)
    return lax.all_to_all(many, axis, 0, 0, axis_index_groups=groups)


def swap_far(value, axis, third, thirds, per_device):
    if len(thirds) == 1:
        return swap(value, axis, thirds[0] // per_device)
    index = sum((third > t).astype(jnp.int32) for t in thirds[:-1])
    ways = [functools.partial(swap, axis=axis, mask=t // per_device) for t in thirds]
    return lax.switch(index, ways, value)


class Plan:
    count, third_bit, top_bit = 8, 2, 4

    def __init__(self, thirds, top, row_blocks, col_blocks):
        third = thirds[0]
        self.third, self.thirds, self.top = third, thirds, top
        self.values = [(m & 1) + (m >> 1 & 1) * third + (m >> 2) * top for m in range(self.count)]
        self.row_blocks = row_blocks
        self.col_blocks = col_blocks
        self.row_far = third >= row_blocks
        self.col_far = third >= col_blocks


def coefficients_kernel(count, top, col_blocks, info, angles, out):
    gens = (1, info[5], top)
    rows = 16 * count
    rid = lax.broadcasted_iota(jnp.int32, (rows, top), 0)
    lane = lax.broadcasted_iota(jnp.int32, (rows, top), 1)
    slot = rid & 15
    base = jnp.where(slot < 8, info[3] + slot, info[4] + (slot & (col_blocks - 1)))
    mask = jnp.zeros_like(rid)
    for k, g in enumerate(gens):
        mask = mask | (((rid >> (4 + k)) & 1) * g)
    block = base ^ mask
    own, other, delays = [], [], []
    for section in range(3):
        d = info[section]
        source = (block & ~d) & (top - 1)
        pick = (source == lane).astype(jnp.float32)
        theta = angles[section * top : (section + 1) * top, :]
        low = (block[:, :1] & d) == 0
        cos = jnp.dot(pick, jnp.cos(theta), precision=HIGHEST, preferred_element_type=jnp.float32)
        sin = jnp.dot(pick, jnp.sin(theta), precision=HIGHEST, preferred_element_type=jnp.float32)
        sin = jnp.where(low, -sin, sin)
        own.append([cos[16 * m : 16 * m + 16] for m in range(count)])
        other.append([sin[16 * m : 16 * m + 16] for m in range(count)])
        delays.append(d)

    def partner(values, d, m):
        result = values[m ^ 1]
        for k, g in enumerate(gens[1:], 1):
            result = jnp.where(d == g, values[m ^ (1 << k)], result)
        return result

    one = jnp.ones((16, 128), jnp.float32)
    zero = jnp.zeros((16, 128), jnp.float32)

    def row_of(start):
        values = [one if m == start else zero for m in range(count)]
        for section in (2, 1, 0):
            a, b, d = own[section], other[section], delays[section]
            scaled = [values[m] * b[m] for m in range(count)]
            values = [values[m] * a[m] + partner(scaled, d, m) for m in range(count)]
        return values

    def col_of():
        values = [one if m == 0 else zero for m in range(count)]
        for section in (0, 1, 2):
            a, b, d = own[section], other[section], delays[section]
            values = [values[m] * a[m] + b[m] * partner(values, d, m) for m in range(count)]
        return values

    for n, values in enumerate(
        (row_of(0), row_of(Plan.top_bit), col_of(), row_of(Plan.third_bit),
         row_of(Plan.top_bit | Plan.third_bit))
    ):
        for m in range(count):
            out[n, m] = values[m]


def coefficients(top, col_blocks, info, angles):
    return pl.pallas_call(
        functools.partial(coefficients_kernel, Plan.count, top, col_blocks),
        out_shape=jax.ShapeDtypeStruct((5, Plan.count, 16, 128), jnp.float32),
        in_specs=[SMEM, VMEM],
        out_specs=VMEM,
        compiler_params=pltpu.CompilerParams(vmem_limit_bytes=32 * 2**20),
    )(info, angles)


def row_kernel(plan, height, near_ref, top_ref, coef_ref, *outs, rows=slice(0, 8)):
    tables = [0, 3]
    blocks = height // 128
    far = plan.third_bit if plan.row_far else 0
    for which, out in enumerate(outs):
        table = tables[which]
        columns = [jnp.transpose(coef_ref[table, m, rows, :]) for m in range(plan.count)]
        for j in range(blocks):
            total = None
            for m in range(plan.count):
                if m & far:
                    continue
                ref = top_ref if m & plan.top_bit else near_ref
                value = plan.values[m] & ~plan.top
                i = j ^ value
                term = ref[128 * i : 128 * i + 128, :] * columns[m][:, j : j + 1]
                total = term if total is None else total + term
            out[128 * j : 128 * j + 128, :] = total


def mix_rows(plan, near, top, coef, width=128):
    height, all_width = near.shape
    n_out = 2 if plan.row_far else 1
    block = pl.BlockSpec((height, width), lambda i: (0, i))
    shape = jax.ShapeDtypeStruct(near.shape, jnp.float32)
    return pl.pallas_call(
        functools.partial(row_kernel, plan, height),
        grid=(all_width // width,),
        out_shape=[shape] * n_out,
        in_specs=[block, block, VMEM],
        out_specs=[block] * n_out,
        compiler_params=pltpu.CompilerParams(vmem_limit_bytes=48 * 2**20),
    )(near, top, coef)


def col_kernel(plan, *refs):
    if plan.col_far:
        near_ref, far_ref, coef_ref, mine, theirs = refs
    else:
        near_ref, coef_ref, mine, theirs = refs
        far_ref = None
    far = plan.third_bit if plan.col_far else 0
    for which, out in enumerate((mine, theirs)):
        for j in range(plan.col_blocks):
            total = None
            for m in range(plan.count):
                if m & plan.top_bit:
                    continue
                ref = far_ref if m & far else near_ref
                value = plan.values[m] & ~(plan.third if m & far else 0)
                i = j ^ value
                term = ref[:, 128 * i : 128 * i + 128] * coef_ref[which, m, 8 + j : 9 + j, :]
                total = term if total is None else total + term
            out[:, 128 * j : 128 * j + 128] = total


def mix_cols(plan, parts, coef, strip=128):
    height, width = parts[0].shape
    block = pl.BlockSpec((strip, width), lambda i: (i, 0))
    shape = jax.ShapeDtypeStruct((height, width), jnp.float32)
    return pl.pallas_call(
        functools.partial(col_kernel, plan),
        grid=(height // strip,),
        out_shape=[shape] * 2,
        in_specs=[block] * len(parts) + [VMEM],
        out_specs=[block] * 2,
        compiler_params=pltpu.CompilerParams(vmem_limit_bytes=48 * 2**20),
    )(*parts, coef)


def deep_kernel(plan, place, field_ref, coef_ref, out_ref):
    tables = (0, 3, 1, 4)
    for to in range(4):
        for j in range(plan.col_blocks):
            total = None
            for m in range(plan.count):
                i = j ^ (m & 1)
                term = field_ref[place[0] ^ (m >> 1), :, 128 * i : 128 * i + 128]
                term = term * coef_ref[tables[to], m, 8 + j : 9 + j, :]
                total = term if total is None else total + term
            out_ref[place[0] ^ to, :, 128 * j : 128 * j + 128] = total


def mix_deep(plan, place, field, coef, strip=64):
    count, height, width = field.shape
    block = pl.BlockSpec((count, strip, width), lambda i: (0, i, 0))
    return pl.pallas_call(
        functools.partial(deep_kernel, plan),
        grid=(height // strip,),
        out_shape=jax.ShapeDtypeStruct(field.shape, jnp.float32),
        in_specs=[SMEM, block, VMEM],
        out_specs=block,
        compiler_params=pltpu.CompilerParams(vmem_limit_bytes=48 * 2**20),
    )(place, field, coef)


def near_kernel(plan, near_ref, top_ref, coef_ref, mine, theirs, middle):
    blocks = near_ref.shape[0] // QUANTUM
    rows = pl.ds(pl.program_id(0) * blocks, blocks)
    row_kernel(plan, near_ref.shape[0], near_ref, top_ref, coef_ref, middle, rows=rows)
    col_kernel(plan, middle, coef_ref, mine, theirs)


def mix_near(plan, near, top, coef):
    height, width = near.shape
    block = pl.BlockSpec((height // 2, width), lambda i: (i, 0))
    shape = jax.ShapeDtypeStruct((height, width), jnp.float32)
    return pl.pallas_call(
        functools.partial(near_kernel, plan),
        grid=(2,),
        out_shape=[shape] * 2,
        in_specs=[block, block, pl.BlockSpec(coef.shape, lambda i: (0, 0, 0, 0))],
        out_specs=[block] * 2,
        scratch_shapes=[pltpu.VMEM((height // 2, width), jnp.float32)],
        compiler_params=pltpu.CompilerParams(vmem_limit_bytes=48 * 2**20),
    )(near, top, coef)


def dot(a, b, over=((1,), (0,))):
    return lax.dot_general(
        a, b, (over, ((), ())), precision=HIGHEST, preferred_element_type=jnp.float32
    )


def inverse_factor(block):
    n = block.shape[0]
    i = lax.broadcasted_iota(jnp.int32, (8, 2 * n), 0)
    lane = lax.broadcasted_iota(jnp.int32, (8, 2 * n), 1)
    unit = [jnp.where(lane == i + 8 * t + n, 1.0, 0.0) for t in range(n // 8)]
    wide = jnp.concatenate([block, jnp.zeros_like(block)], axis=1)
    tiles = [wide[8 * t : 8 * t + 8] + unit[t] for t in range(n // 8)]
    for j in range(n):
        first, r = divmod(j, 8)
        row = tiles[first][r : r + 1, :]
        scaled = row * (1.0 / row[:, j : j + 1])
        for t in range(first, n // 8):
            col = tiles[t][:, j : j + 1]
            if t == first:
                col = jnp.where(i[:, :1] > r, col, 0.0)
            tiles[t] = tiles[t] - col * scaled
    out = []
    for t in range(n // 8):
        pivot = jnp.sum(jnp.where(lane == i + 8 * t, tiles[t], 0.0), axis=1, keepdims=True)
        out.append(tiles[t][:, n:] * lax.rsqrt(pivot))
    return jnp.concatenate(out, axis=0)


def weights_kernel(square, given, out, work, right):
    size, n = square.shape[0], 64
    work[...] = square[...]
    right[...] = given[...]
    inverses = []
    for k in range(0, size, n):
        inverse = inverse_factor(work[k : k + n, k : k + n])
        inverses.append(inverse)
        mine = dot(inverse, right[k : k + n, :])
        right[k : k + n, :] = mine
        if k + n < size:
            below = dot(work[k + n :, k : k + n], inverse, ((1,), (1,)))
            work[k + n :, k : k + n] = below
            work[k + n :, k + n :] -= dot(below, below, ((1,), (1,)))
            right[k + n :, :] -= dot(below, mine)
    for k in range(size - n, -1, -n):
        rest = right[k : k + n, :]
        if k + n < size:
            rest = rest - dot(work[k + n :, k : k + n], out[k + n :, :], ((0,), (0,)))
        out[k : k + n, :] = dot(inverses[k // n], rest, ((0,), (0,)))


def solve_weights(square, given):
    return pl.pallas_call(
        weights_kernel,
        out_shape=jax.ShapeDtypeStruct(given.shape, jnp.float32),
        in_specs=[VMEM, VMEM],
        out_specs=VMEM,
        scratch_shapes=[
            pltpu.VMEM(square.shape, jnp.float32),
            pltpu.VMEM(given.shape, jnp.float32),
        ],
        compiler_params=pltpu.CompilerParams(vmem_limit_bytes=32 * 2**20),
    )(square, given)


def selection(coef, base, n_blocks, first, third, top, panel):
    n = n_blocks * QUANTUM
    ids = base * QUANTUM + jnp.arange(n, dtype=jnp.int32)
    slots = jnp.arange(2 * PANEL, dtype=jnp.int32)
    chosen = panel + jnp.where(slots < PANEL, slots, top * QUANTUM + slots - PANEL)
    result = jnp.zeros((2 * PANEL, n), jnp.float32)
    for m in range(Plan.count):
        at = ids ^ (((m & 1) + (m >> 1 & 1) * third + (m >> 2) * top) * QUANTUM)
        weight = coef[2, m, first : first + n_blocks].reshape(n)
        result = result + jnp.where(at[None, :] == chosen[:, None], weight[None, :], 0.0)
    return result


def transposed(value):
    n_row, n_col = lax.axis_size("row"), lax.axis_size("col")
    cores = n_col // (Z_HI * Y)
    pairs = []
    for r in range(n_row):
        x, z_lo = divmod(r, Z_LO)
        for c in range(n_col):
            z_hi, y, core = c // cores // Y, c // cores % Y, c % cores
            to = (z_hi * Z_LO + y) * n_col + (z_lo * Y + x) * cores + core
            pairs.append((r * n_col + c, to))
    return lax.ppermute(value, ("row", "col"), pairs)


def mix_piece(plan, piece, top_piece, coef, third):
    moved = {0: piece, plan.top_bit: top_piece}
    far, far_value = plan.top_bit, plan.top
    if plan.col_far:
        pair = jnp.concatenate([piece, top_piece])
        pair = swap_far(pair, "col", third, plan.thirds, plan.col_blocks)
        moved[plan.third_bit] = pair[: piece.shape[0]]
        moved[plan.third_bit | plan.top_bit] = pair[piece.shape[0] :]
        far, far_value = far | plan.third_bit, far_value | plan.third
    mixed = []
    for j in range(plan.col_blocks):
        total = 0.0
        for m in range(plan.count):
            i = j ^ (plan.values[m] & ~far_value)
            source = moved[m & far][:, 128 * i : 128 * i + 128]
            total = total + source * coef[0, m, 8 + j][None, :]
        mixed.append(total)
    return jnp.concatenate(mixed, axis=1)


def mix_field(plan, covariance, over, coef, third):
    if not plan.col_far:
        return mix_near(plan, covariance, over, coef)
    if plan.row_far:
        mine, theirs = mix_rows(plan, covariance, over, coef)
        field = mine + swap_far(theirs, "row", third, plan.thirds, plan.row_blocks)
    else:
        (field,) = mix_rows(plan, covariance, over, coef)
    parts = [field, swap_far(field, "col", third, plan.thirds, plan.col_blocks)]
    return mix_cols(plan, parts, coef)


def shards(covariance, angles, delays, panel):
    rows_dev, cols_dev = covariance.shape
    n_row = lax.axis_size("row")
    row_blocks, col_blocks = rows_dev // QUANTUM, cols_dev // QUANTUM
    top = row_blocks * n_row // 2
    given = jnp.sum(delays) // QUANTUM - top - 1
    thirds = [1 << n for n in range(1, top.bit_length() - 1)]
    near = [t for t in thirds if t < min(row_blocks, col_blocks)]
    side = [t for t in thirds if col_blocks <= t < row_blocks]
    cores = lax.axis_size("col") // (Z_HI * Y)
    inner_z = col_blocks * cores * Y
    away = [t for t in thirds if max(row_blocks, col_blocks) <= t < inner_z]
    deep = [t for t in thirds if t >= inner_z]
    plans = [Plan(group, top, row_blocks, col_blocks) for group in (near, side, away, deep)]
    inner = (given > 1) & (given < top)
    third = jnp.where(inner, given, near[0])
    index = sum((third >= group[0]).astype(jnp.int32) for group in (side, away, deep))
    rb = lax.axis_index("row").astype(jnp.int32) * row_blocks
    cb = lax.axis_index("col").astype(jnp.int32) * col_blocks
    info = jnp.concatenate([delays // QUANTUM, rb[None], cb[None], third[None]]).astype(jnp.int32)
    coef = coefficients(top, col_blocks, info, angles.reshape(3 * top, QUANTUM))

    sel_r = selection(coef, rb, row_blocks, 0, third, top, panel[0])
    sel_c = selection(coef, cb, col_blocks, 8, third, top, panel[0])
    part = jnp.dot(sel_r, covariance, precision=HIGHEST)
    spread = lax.all_to_all(part.reshape(n_row, -1, cols_dev), "row", 0, 0)
    over = swap(covariance, "row", top // row_blocks)
    piece = jnp.sum(spread, axis=0)
    block = jnp.dot(piece, sel_c.T, precision=HIGHEST)
    along = gather(jnp.concatenate([piece, block], axis=1), "col", cores * Y, Z_HI)
    z_hi = lax.axis_index("col") // (cores * Y)
    apart = top // col_blocks // (cores * Y)
    top_piece = lax.dynamic_index_in_dim(along, z_hi ^ apart, 0, keepdims=False)[:, :cols_dev]
    block = jnp.sum(along[:, :, cols_dev:], axis=0)
    mixed = lax.switch(
        index, [functools.partial(mix_piece, plan) for plan in plans], piece, top_piece, coef, third
    )
    quarter = gather(jnp.concatenate([mixed, block], axis=1), "row", 1, Z_LO)
    quarter = quarter.reshape(-1, cols_dev + 2 * PANEL)
    flipped = transposed(quarter[:, :cols_dev])
    over, quarter, flipped = lax.optimization_barrier((over, quarter, flipped))

    def finish(quarter, flipped):
        pieces = jnp.concatenate([quarter[:, cols_dev:], flipped], axis=1)
        pieces = gather(pieces, "col", cores, Y)
        block = jnp.sum(pieces[:, :, : 2 * PANEL], axis=0)
        block = block + swap(block, "col", 1)
        here = pieces[:, :, 2 * PANEL :].reshape(2 * PANEL, cols_dev)
        twin = swap(here, "col", 1)
        both = gather(jnp.concatenate([quarter[:, :cols_dev], block], axis=1), "row", Z_LO, X)
        both = both.reshape(2 * PANEL, -1)
        weights = solve_weights(both[:, cols_dev:], both[:, :cols_dev])
        low = lax.axis_index("col") % 2 == 0
        columns = jnp.concatenate([jnp.where(low, here, twin), jnp.where(low, twin, here)], axis=1)
        return lax.dot_general(columns, weights, (((0,), (0,)), ((), ())), precision=HIGHEST)

    def close(quarter, flipped):
        def skip(quarter, flipped):
            return jnp.zeros((rows_dev, cols_dev), jnp.float32)

        return lax.cond(panel[0] >= 0, finish, skip, quarter, flipped)

    def plain(covariance, over, quarter, flipped, coef):
        mine, moving = lax.switch(
            index,
            [functools.partial(mix_field, plan) for plan in plans[:3]],
            covariance, over, coef, third,
        )
        arrived = swap(moving, "col", top // col_blocks)
        return mine + arrived - close(quarter, flipped)

    def send(field):
        parts = [lax.dynamic_index_in_dim(field, z_hi ^ k) for k in range(1, Z_HI)]
        return [swap(part, "col", k * cores * Y) for k, part in enumerate(parts, 1)]

    def place(field, parts):
        for k, part in enumerate(parts, 1):
            field = lax.dynamic_update_slice(field, part, (z_hi ^ k, 0, 0))
        return field

    def through(covariance, over, quarter, flipped, coef):
        plan = plans[3]
        mine, theirs = mix_rows(plan, covariance, over, coef)
        field = mine + swap(theirs, "row", plan.third // row_blocks)
        field, quarter, flipped = lax.optimization_barrier((field, quarter, flipped))
        field = field.reshape(Z_HI, -1, cols_dev)
        parts = send(field)
        update = close(quarter, flipped)
        parts, update = lax.optimization_barrier((parts, update))
        field = mix_deep(plan, z_hi.astype(jnp.int32)[None], place(field, parts), coef)
        field = place(field, lax.optimization_barrier(send(field)))
        return field.reshape(rows_dev, cols_dev) - update

    return lax.cond(index == 3, through, plain, covariance, over, quarter, flipped, coef)


def solution(mesh):
    in_specs = (P("row", "col"), P(), P(), P())
    out_specs = P("row", "col")
    return jax.shard_map(shards, mesh=mesh, in_specs=in_specs, out_specs=out_specs, check_vma=False)
```
